256 devices in a mesh: ctx: 32 (over x_lo, z, core), head: 8 (over x_hi, y).
Axes of the slice: x: 4 (x_hi: 2, x_lo: 2; x = x_hi * 2 + x_lo), y: 4, z: 8, core: 2. Of those that a mesh axis runs over, the one named last changes fastest.
Arguments:
- queries: bfloat16 [65536, 4096], P('ctx', 'head'), may hold values from -8 to 8
- key_state_matrix: bfloat16 [65536, 1024], P('ctx', 'head'), may hold values from -4.5 to 4.5
- value_state_matrix: bfloat16 [65536, 1024], P('ctx', 'head'), may hold values from -6 to 6
- selected: int32 [128, 3], P('ctx'), may hold values from -1 to 123, as said below
- out_weight: bfloat16 [4096, 2048], P('head'), may hold values from -0.09375 to 0.09375
Outputs:
- mixed: bfloat16 [65536, 2048], P('ctx', 'head')
The draws below stay inside these ranges and needn't reach their ends.
Inputs may be any that keep to these rules, and one draw needn't show every extreme that they name: `selected`: row j names blocks that lie on lower indices of ctx than block j (the block's index // 4 is the owning index), on three different indices; all rows of one index of ctx name at most one distinct block of each other index; a slot is -1 only when block j's index has fewer than three lower indices, and then exactly the missing slots are -1.
All inputs are finite; a program needn't handle non-finite values.
Results may differ from the reference program's by a relative error of at most 0.015.
Values may be sent and summed in bfloat16 or wider, within the bound.
No kernel may reach another device: no remote copies, remote signals or barrier semaphores. Data moves between devices by JAX's collectives and lax.ppermute only.
A program may use at most 128 MiB of HBM per device.

```python
import jax
import jax.numpy as jnp
from jax import lax

QUERY_HEADS = 32
KEY_VALUE_HEADS = 8
HEAD_SIZE = 128
DOUT = 2048
BLOCK_TOKENS = 512
D = 4096
BLK_DEV = 4
SEQUENCE_TOKENS = 65536
BLOCK_COUNT = 128


def draw_queries(key, part):
    key = jax.random.fold_in(key, 1)
    final_output = jnp.clip(jax.random.normal(key, (SEQUENCE_TOKENS, QUERY_HEADS * HEAD_SIZE), jnp.float32), -4.5, 4.5)
    return final_output.astype(jnp.bfloat16)


def draw_key_state_matrix(key, part):
    key = jax.random.fold_in(key, 2)
    final_output = jnp.clip(jax.random.normal(key, (SEQUENCE_TOKENS, KEY_VALUE_HEADS * HEAD_SIZE), jnp.float32), -4.5, 4.5)
    return final_output.astype(jnp.bfloat16)


def draw_selected(key, part):
    key = jax.random.fold_in(key, 3)
    first_key, second_key = jax.random.split(key)
    devices = BLOCK_COUNT // BLK_DEV
    owner = jnp.arange(BLOCK_COUNT) // BLK_DEV
    slots = jnp.arange(devices)
    noise = jax.random.randint(first_key, (BLOCK_COUNT, devices), 0, 1 << 20)
    ranking = noise * devices + slots[None, :]
    forced = (owner[:, None] == devices - 1) & (slots[None, :] == devices - 2)
    ranking = jnp.where(forced, -1, ranking)
    earlier = slots[None, :] < owner[:, None]
    ranking = jnp.where(earlier, ranking, (1 << 30) + slots[None, :])
    picked = jnp.argsort(ranking, axis=1, stable=True)[:, :3]
    within = jax.random.randint(second_key, (devices, devices), 0, BLK_DEV)
    within = within.at[devices - 1, devices - 2].set(BLK_DEV - 1)
    inner = within[owner[:, None], picked]
    final_output = jnp.where(picked < owner[:, None], picked * BLK_DEV + inner, -1)
    return final_output.astype(jnp.int32)


def level_of(key, dims, cuts, low, high):
    level, own = 1.0, jax.random.fold_in(key, 6)
    for dim, shards_of in cuts:
        steps = jnp.exp(jax.random.uniform(jax.random.fold_in(own, dim), (shards_of,), jnp.float32, low / len(cuts), high / len(cuts)))
        level = level * jnp.repeat(steps, dims[dim] // shards_of).reshape([-1 if axis == dim else 1 for axis in range(len(dims))])
    return level


def centred(key, extent, scale, most, pieces=(), held_as=jnp.bfloat16):
    values = jax.random.normal(key, extent, jnp.float32) * scale
    if len(pieces) > 0:
        values = level_of(key, extent, pieces, -0.22, 0.18) * values
    return jnp.clip(values, min=-most, max=most).astype(held_as)


def setup_inputs(seed: int = 0) -> dict:
    seeds = jax.random.split(jax.random.key(seed), 6)
    return {
        "queries": draw_queries(jax.random.fold_in(seeds[5], 71), 0),
        "key_state_matrix": draw_key_state_matrix(jax.random.fold_in(seeds[5], 71), 0),
        "value_state_matrix": centred(seeds[2], (SEQUENCE_TOKENS, KEY_VALUE_HEADS * HEAD_SIZE), 1.0, 6.0, ((0, 32), (1, 8))),
        "selected": draw_selected(jax.random.fold_in(seeds[5], 71), 0),
        "out_weight": centred(seeds[4], (D, DOUT), D ** -0.5, 0.09375, ((0, 8),)),
    }


def reference(queries, key_state_matrix, value_state_matrix, selected, out_weight):
    query_group_size = QUERY_HEADS // KEY_VALUE_HEADS
    score_scale = HEAD_SIZE ** -0.5
    blocked_queries = queries.reshape(BLOCK_COUNT, BLOCK_TOKENS, KEY_VALUE_HEADS, query_group_size, HEAD_SIZE)
    blocked_keys = key_state_matrix.reshape(BLOCK_COUNT, BLOCK_TOKENS, KEY_VALUE_HEADS, HEAD_SIZE)
    blocked_values = value_state_matrix.reshape(BLOCK_COUNT, BLOCK_TOKENS, KEY_VALUE_HEADS, HEAD_SIZE)
    causal = jnp.arange(BLOCK_TOKENS)[:, None] >= jnp.arange(BLOCK_TOKENS)[None, :]

    def one_block(index):
        chosen_row = selected[index]
        picked_block_list = jnp.concatenate([index[None].astype(jnp.int32), jnp.maximum(chosen_row, 0).astype(jnp.int32)])
        gathered_keys = blocked_keys[picked_block_list].reshape(4 * BLOCK_TOKENS, KEY_VALUE_HEADS, HEAD_SIZE).astype(jnp.float32)
        gathered_values = blocked_values[picked_block_list].reshape(4 * BLOCK_TOKENS, KEY_VALUE_HEADS, HEAD_SIZE).astype(jnp.float32)
        live_sel = jnp.broadcast_to(jnp.repeat(chosen_row >= 0, BLOCK_TOKENS)[None, :], (BLOCK_TOKENS, 3 * BLOCK_TOKENS))
        live = jnp.concatenate([causal, live_sel], axis=1)
        query_here = blocked_queries[index].astype(jnp.float32)
        scores = jnp.einsum('qhgd,khd->hgqk', query_here, gathered_keys) * score_scale
        scores = jnp.where(live[None, None], scores, -1e30)
        highest = jnp.max(scores, axis=-1, keepdims=True)
        expon = jnp.exp(scores - highest)
        weights = (expon / jnp.sum(expon, axis=-1, keepdims=True)).astype(jnp.bfloat16)
        output = jnp.einsum('hgqk,khd->qhgd', weights.astype(jnp.float32), gathered_values)
        return output.reshape(BLOCK_TOKENS, QUERY_HEADS * HEAD_SIZE).astype(jnp.bfloat16)

    attended = lax.map(one_block, jnp.arange(BLOCK_COUNT, dtype=jnp.int32)).reshape(SEQUENCE_TOKENS, QUERY_HEADS * HEAD_SIZE)
    return jnp.dot(attended, out_weight, preferred_element_type=jnp.float32).astype(jnp.bfloat16)
```

```python
import functools

import jax
import jax.numpy as jnp
from jax import lax
from jax.experimental import pallas as pl
from jax.experimental.pallas import tpu as pltpu
from jax.sharding import PartitionSpec as P

HEAD_SIZE = 128
BLOCK_TOKENS = 512
TILE = 256
SLOTS = 4
SCORE_SCALE = HEAD_SIZE ** (-0.5)
EXP2_SCALE = SCORE_SCALE * 1.4426950408889634


def attention_kernel(q_heads, table, q_ref, kv_ref, o_ref, keys, values, sems):
    step = pl.program_id(0)
    steps = pl.num_programs(0)
    here = lax.rem(step, 2)

    def copies(at, buf):
        out = []
        for slot in range(SLOTS):
            own = table[at * SLOTS + SLOTS - 1]
            block = table[at * SLOTS + slot]
            block = jnp.where(block < 0, own, block)
            rows = pl.ds(pl.multiple_of(block * BLOCK_TOKENS, BLOCK_TOKENS), BLOCK_TOKENS)
            to = pl.ds(slot * BLOCK_TOKENS, BLOCK_TOKENS)
            out.append(
                pltpu.make_async_copy(
                    kv_ref.at[rows, pl.ds(0, HEAD_SIZE)], keys.at[buf, to], sems.at[buf, slot, 0]
                )
            )
            out.append(
                pltpu.make_async_copy(
                    kv_ref.at[rows, pl.ds(HEAD_SIZE, HEAD_SIZE)],
                    values.at[buf, to, pl.ds(0, HEAD_SIZE)],
                    sems.at[buf, slot, 1],
                )
            )
        return out

    @pl.when(step == 0)
    def _():
        for copy in copies(step, here):
            copy.start()

    @pl.when(step + 1 < steps)
    def _():
        for copy in copies(step + 1, 1 - here):
            copy.start()

    for copy in copies(step, here):
        copy.wait()

    values[here, pl.ds(0, SLOTS * BLOCK_TOKENS), pl.ds(HEAD_SIZE, HEAD_SIZE)] = jnp.ones(
        (SLOTS * BLOCK_TOKENS, HEAD_SIZE), jnp.bfloat16
    )
    for slot in range(SLOTS - 1):

        @pl.when(table[step * SLOTS + slot] < 0)
        def _():
            to = pl.ds(slot * BLOCK_TOKENS, BLOCK_TOKENS)
            first = keys[here, pl.ds((SLOTS - 1) * BLOCK_TOKENS, 16), :][0:1, :]
            keys[here, to, :] = jnp.broadcast_to(first, (BLOCK_TOKENS, HEAD_SIZE))
            values[here, to, :] = jnp.zeros((BLOCK_TOKENS, 2 * HEAD_SIZE), jnp.bfloat16)

    row = lax.broadcasted_iota(jnp.int32, (TILE, TILE), 0)
    col = lax.broadcasted_iota(jnp.int32, (TILE, TILE), 1)
    causal = row >= col
    dims = (((1,), (1,)), ((), ()))

    for head in range(q_heads):
        lanes = pl.ds(head * HEAD_SIZE, HEAD_SIZE)
        for tile in range(BLOCK_TOKENS // TILE):
            rows = pl.ds(tile * TILE, TILE)
            full = (SLOTS - 1) * BLOCK_TOKENS + tile * TILE
            query = q_ref[rows, lanes]
            far = lax.dot_general(
                query, keys[here, pl.ds(0, full), :], dims, preferred_element_type=jnp.float32
            )
            near = lax.dot_general(
                query, keys[here, pl.ds(full, TILE), :], dims, preferred_element_type=jnp.float32
            )
            near = jnp.where(causal, near, -1e30)
            highest = jnp.maximum(
                jnp.max(far, axis=1, keepdims=True), jnp.max(near, axis=1, keepdims=True)
            )
            far = jnp.exp2((far - highest) * EXP2_SCALE).astype(jnp.bfloat16)
            near = jnp.exp2((near - highest) * EXP2_SCALE).astype(jnp.bfloat16)
            total = jnp.dot(
                far, values[here, pl.ds(0, full), :], preferred_element_type=jnp.float32
            ) + jnp.dot(
                near, values[here, pl.ds(full, TILE), :], preferred_element_type=jnp.float32
            )
            o_ref[rows, lanes] = (total[:, :HEAD_SIZE] / total[:, HEAD_SIZE:]).astype(jnp.bfloat16)


def attention(queries, gathered, table):
    rows, width = queries.shape
    blocks = rows // BLOCK_TOKENS
    keys = SLOTS * BLOCK_TOKENS
    return pl.pallas_call(
        functools.partial(attention_kernel, width // HEAD_SIZE),
        out_shape=jax.ShapeDtypeStruct((rows, width), jnp.bfloat16),
        grid_spec=pltpu.PrefetchScalarGridSpec(
            num_scalar_prefetch=1,
            grid=(blocks,),
            in_specs=[
                pl.BlockSpec((BLOCK_TOKENS, width), lambda i, t: (i, 0)),
                pl.BlockSpec(memory_space=pl.ANY),
            ],
            out_specs=pl.BlockSpec((BLOCK_TOKENS, width), lambda i, t: (i, 0)),
            scratch_shapes=[
                pltpu.VMEM((2, keys, HEAD_SIZE), jnp.bfloat16),
                pltpu.VMEM((2, keys, 2 * HEAD_SIZE), jnp.bfloat16),
                pltpu.SemaphoreType.DMA((2, SLOTS, 2)),
            ],
        ),
        compiler_params=pltpu.CompilerParams(
            dimension_semantics=("arbitrary",), vmem_limit_bytes=48 * 1024 * 1024
        ),
        cost_estimate=pl.CostEstimate(
            flops=4 * rows * (width // HEAD_SIZE) * keys * HEAD_SIZE,
            bytes_accessed=4 * rows * width + 4 * blocks * keys * HEAD_SIZE,
            transcendentals=rows * (width // HEAD_SIZE) * keys,
        ),
    )(table, queries, gathered)


def project_kernel(parts, a_ref, w_ref, o_ref):
    total = jnp.dot(a_ref[0], w_ref[0], preferred_element_type=jnp.float32)
    for part in range(1, parts):
        total += jnp.dot(a_ref[part], w_ref[part], preferred_element_type=jnp.float32)
    o_ref[0] = total.astype(jnp.bfloat16)


def project(attended, weight):
    parts, rows, features = attended.shape
    columns = weight.shape[2] // parts
    return pl.pallas_call(
        functools.partial(project_kernel, parts),
        out_shape=jax.ShapeDtypeStruct((parts, rows, columns), jnp.bfloat16),
        grid=(parts,),
        in_specs=[
            pl.BlockSpec((parts, rows, features), lambda i: (0, 0, 0)),
            pl.BlockSpec((parts, features, columns), lambda i: (0, 0, i)),
        ],
        out_specs=pl.BlockSpec((1, rows, columns), lambda i: (i, 0, 0)),
        compiler_params=pltpu.CompilerParams(
            dimension_semantics=("arbitrary",), vmem_limit_bytes=32 * 1024 * 1024
        ),
        cost_estimate=pl.CostEstimate(
            flops=2 * parts * parts * rows * features * columns,
            bytes_accessed=2 * parts * parts * features * columns + 4 * parts * rows * features,
            transcendentals=0,
        ),
    )(attended, weight)


def gather_weight(out_weight, ctx_count):
    half = out_weight.shape[0] // 2
    core = lax.rem(lax.axis_index("ctx"), 2)
    head = lax.axis_index("head")
    mine = lax.dynamic_slice_in_dim(out_weight, core * half, half, 0)

    def along(dx, dy):
        return [
            (i, ((i // 4 + dx) % 2) * 4 + (i % 4 + dy) % 4) for i in range(8)
        ]

    def send(value, dx, dy):
        return lax.ppermute(value, "head", along(dx, dy))

    other = send(mine, 1, 0)
    mine_up, mine_down = send(mine, 0, 1), send(mine, 0, -1)
    other_up, other_down = send(other, 0, 1), send(other, 0, -1)
    mine_far, other_far = send(mine_up, 0, 1), send(other_down, 0, -1)
    pieces = [mine, mine_up, mine_far, mine_down, other, other_up, other_far, other_down]
    stacked = jnp.stack(pieces)
    swapped = lax.ppermute(stacked, "ctx", [(i, i ^ 1) for i in range(ctx_count)])
    both = jnp.concatenate([stacked, swapped])
    owner = jnp.arange(8)
    dx = jnp.where(owner // 4 == head // 4, 0, 1)
    dy = (head % 4 - owner % 4) % 4
    which = dx * 4 + dy
    order = jnp.stack(
        [jnp.where(core == 0, which, which + 8), jnp.where(core == 0, which + 8, which)], axis=1
    ).reshape(16)
    return both[order].reshape(8, 2 * half, out_weight.shape[1])


def per_device(queries, key_state_matrix, value_state_matrix, selected, out_weight):
    ctx_count = lax.axis_size("ctx")
    head_count = lax.axis_size("head")
    ctx_index = lax.axis_index("ctx")
    rows, width = queries.shape
    blocks = rows // BLOCK_TOKENS
    stacked = jnp.concatenate([key_state_matrix, value_state_matrix], axis=1)
    gathered = lax.all_gather(stacked, "ctx", axis=0, tiled=True)
    weight = gather_weight(out_weight, ctx_count)
    own = (ctx_index * blocks + jnp.arange(blocks, dtype=jnp.int32))[:, None]
    table = jnp.concatenate([selected, own], axis=1).reshape(-1)
    attended = attention(queries, gathered, table)
    tokens = lax.all_to_all(
        attended.reshape(head_count, rows // head_count, width), "head", 0, 0, tiled=True
    )
    mixed = project(tokens, weight)
    return lax.all_to_all(mixed, "head", 0, 0, tiled=True).reshape(rows, -1)


def solution(mesh):
    return jax.shard_map(
        per_device,
        mesh=mesh,
        in_specs=(
            P("ctx", "head"),
            P("ctx", "head"),
            P("ctx", "head"),
            P("ctx", None),
            P("head", None),
        ),
        out_specs=P("ctx", "head"),
        check_vma=False,
    )
```

```python
import functools

import jax
import jax.numpy as jnp
import numpy as np
from jax import lax
from jax.experimental import pallas as pl
from jax.experimental.pallas import tpu as pltpu
from jax.sharding import PartitionSpec as P

HEAD_SIZE = 128
BLOCK_TOKENS = 512
TILE = 256
SLOTS = 4
BLOCKS = 4
ROWS = BLOCKS * BLOCK_TOKENS
RING = 8
CORES = 4 * RING
EXP2_SCALE = HEAD_SIZE ** (-0.5) * 1.4426950408889634

SCHEDULE = (
    (
        (
            0, 1, 2, 3, 4, -1, 6, -1, 8, -1, 10, -1, 12, -1, 14, -1,
            16, 17, 18, 19, 20, -1, 22, -1, 24, -1, 26, -1, 28, -1, -1, -1,
        ),
        (
            -1, 1, -1, 3, -1, 5, -1, 7, -1, 9, -1, 11, -1, 13, -1, 15,
            -1, -1, -1, -1, -1, -1, -1, -1, -1, -1, -1, -1, -1, -1, -1, -1,
        ),
    ),
    (
        (
            1, 0, 3, 2, 5, -1, 7, -1, 9, -1, 11, -1, 13, -1, 15, -1,
            17, 16, 19, 18, 21, -1, 23, -1, 25, -1, 27, -1, 29, -1, -1, -1,
        ),
        (
            -1, 0, -1, 2, -1, 4, -1, 6, -1, 8, -1, 10, -1, 12, -1, 14,
            -1, -1, -1, -1, -1, -1, -1, -1, -1, -1, -1, -1, -1, -1, -1, -1,
        ),
    ),
    (
        (
            -1, 3, 0, -1, 2, -1, 4, -1, 6, -1, 8, -1, 10, -1, -1, 1,
            -1, 1, 16, 3, 18, 5, 20, 7, 22, 9, 24, 11, 26, 13, -1, 15,
        ),
        (
            14, -1, 0, -1, 2, -1, 4, -1, 6, -1, 8, -1, 10, -1, 12, -1,
            -1, -1, -1, -1, -1, -1, -1, -1, -1, -1, -1, -1, -1, -1, -1, -1,
        ),
    ),
    (
        (
            -1, 2, 1, -1, 3, -1, 5, -1, 7, -1, 9, -1, 11, -1, -1, 0,
            -1, 18, 17, 2, 19, 4, 21, 6, 23, 8, 25, 10, 27, 12, -1, 14,
        ),
        (
            15, -1, 1, -1, 3, -1, 5, -1, 7, -1, 9, -1, 11, -1, 13, -1,
            -1, -1, -1, -1, -1, -1, -1, -1, -1, -1, -1, -1, -1, -1, -1, -1,
        ),
    ),
    (
        (
            -1, -1, -1, -1, 0, -1, 2, -1, 4, -1, 6, -1, 8, 1, -1, 3,
            14, 19, -1, 5, 16, 7, 18, 9, 20, 11, 22, 13, 24, 15, 12, 1,
        ),
        (
            -1, -1, -1, -1, 0, -1, 2, -1, 4, -1, 6, -1, 8, -1, 10, -1,
            -1, -1, -1, -1, -1, -1, -1, -1, -1, -1, -1, -1, -1, -1, -1, -1,
        ),
    ),
    (
        (
            -1, -1, -1, -1, 1, -1, 3, -1, 5, -1, 7, -1, 9, 0, -1, 2,
            15, 0, -1, 4, 17, 6, 19, 8, 21, 10, 23, 12, 25, 14, 13, 16,
        ),
        (
            -1, -1, -1, -1, 1, -1, 3, -1, 5, -1, 7, -1, -1, 0, 11, -1,
            -1, -1, -1, -1, -1, -1, -1, -1, -1, -1, -1, -1, -1, -1, -1, -1,
        ),
    ),
    (
        (
            -1, -1, -1, -1, -1, -1, 0, -1, 2, -1, 4, 1, 6, 3, -1, -1,
            12, 5, 14, 7, 0, 9, 16, 11, 18, 13, 20, 15, 22, 1, 10, 19,
        ),
        (
            -1, -1, -1, -1, -1, -1, -1, -1, 2, -1, 4, -1, -1, 3, 8, -1,
            -1, -1, -1, -1, -1, -1, -1, -1, -1, -1, -1, -1, -1, -1, -1, -1,
        ),
    ),
    (
        (
            -1, -1, -1, -1, -1, -1, -1, -1, -1, -1, 5, -1, 7, -1, -1, -1,
            13, 4, 15, 6, -1, 8, 17, 10, 5, 12, 21, 14, 23, 16, 11, 17,
        ),
        (
            -1, -1, -1, -1, -1, -1, 1, -1, 3, -1, -1, 0, 7, -1, 9, -1,
            -1, -1, -1, -1, -1, -1, -1, -1, -1, -1, -1, -1, -1, -1, -1, -1,
        ),
    ),
    (
        (
            -1, -1, -1, -1, -1, -1, -1, -1, -1, -1, -1, -1, 4, -1, -1, -1,
            10, 2, 12, 9, 14, 11, 0, 13, 2, 15, 18, -1, 20, 19, 8, 5,
        ),
        (
            -1, -1, -1, -1, -1, -1, -1, -1, -1, 1, -1, 3, 6, -1, -1, 3,
            -1, -1, -1, -1, -1, -1, -1, -1, -1, -1, -1, -1, -1, -1, -1, -1,
        ),
    ),
    (
        (
            -1, -1, -1, -1, -1, -1, -1, -1, -1, -1, -1, -1, 5, -1, -1, -1,
            -1, 6, -1, -1, -1, -1, -1, -1, 17, -1, 9, -1, 21, -1, -1, 4,
        ),
        (
            -1, -1, -1, -1, -1, -1, -1, -1, -1, -1, -1, -1, -1, 2, 7, -1,
            -1, -1, -1, -1, -1, -1, -1, -1, -1, -1, -1, -1, -1, -1, -1, -1,
        ),
    ),
)
CHECKPOINTS = (5, 7, 9)
COST = 12


def target(way, core):
    if way == 1:
        return core + CORES // 2
    side, place = divmod(core, CORES // 2)
    return side * (CORES // 2) + (place + (2 if core % 2 == 0 else -2)) % (CORES // 2)


def plan():
    found = [{core: "own", core ^ 1: "other"} for core in range(CORES)]
    for step, sends in enumerate(SCHEDULE):
        for way, row in enumerate(sends):
            for core, owner in enumerate(row):
                if owner >= 0:
                    found[target(way, core)].setdefault(owner, (step, way))
    return found


def batches(found):
    out = []
    for number, last in enumerate(CHECKPOINTS):
        first = -2 if number == 0 else CHECKPOINTS[number - 1]
        out.append(
            [
                [
                    owner
                    for owner, place in sorted(held.items())
                    if (owner // 2 < core // 2 or owner == core ^ 1)
                    and first < (-1 if isinstance(place, str) else place[0]) <= last
                ]
                for core, held in enumerate(found)
            ]
        )
    return out


def start_from(refs, numbers, source, first, rows, to, sem):
    for number in numbers:

        @pl.when(source == number)
        def _():
            at = pl.ds(pl.multiple_of(first, BLOCK_TOKENS), rows)
            pltpu.make_async_copy(refs[number].at[at], to, sem).start()


def wait_for(refs, source, rows, to, sem):
    @pl.when(source >= 0)
    def _():
        pltpu.make_async_copy(refs[0].at[pl.ds(0, rows)], to, sem).wait()


def move_kernel(ways, way_base, slots, slot_base, row, want, *refs):
    outs = len(ways) + (2 if slots else 0)
    ins, outs, sems = refs[: -outs - 1], refs[-outs - 1 : -1], refs[-1]

    def block_of(slot, which):
        owner = row[slot_base + 2 * slot]
        block = jnp.where(owner >= 0, want[which * CORES + jnp.maximum(owner, 0)], -1)
        source = jnp.where(block >= 0, row[slot_base + 2 * slot + 1], -1)
        return source, jnp.maximum(block, 0) * BLOCK_TOKENS

    jobs = [(numbers, row[way_base + i], 0, ROWS, outs[i]) for i, numbers in enumerate(ways)]
    for slot, numbers in enumerate(slots):
        for which in range(2):
            source, first = block_of(slot, which)
            jobs.append((numbers, source, first, BLOCK_TOKENS, outs[len(ways) + which].at[slot]))
    for i, (numbers, source, first, rows, to) in enumerate(jobs):
        start_from(ins, numbers, source, first, rows, to, sems.at[i])
    for i, (numbers, source, first, rows, to) in enumerate(jobs):
        wait_for(ins, source, rows, to, sems.at[i])


def move(ways, slots, scalars, arrays, width, after=()):
    out_shapes = [(ROWS, width)] * len(ways[0]) + [(len(slots[0]), BLOCK_TOKENS, width)] * (2 if slots[0] else 0)

    def whole(shape):
        return pl.BlockSpec(shape, lambda *_: (0,) * len(shape))

    return pl.pallas_call(
        functools.partial(move_kernel, *ways, *slots),
        out_shape=[jax.ShapeDtypeStruct(s, arrays[0].dtype) for s in out_shapes],
        grid_spec=pltpu.PrefetchScalarGridSpec(
            num_scalar_prefetch=len(scalars),
            grid=(1,),
            in_specs=[pl.BlockSpec(memory_space=pltpu.HBM)] * (len(arrays) + len(after)),
            out_specs=[whole(s) for s in out_shapes],
            scratch_shapes=[pltpu.SemaphoreType.DMA((len(ways[0]) + 2 * len(slots[0]),))],
        ),
        compiler_params=pltpu.CompilerParams(vmem_limit_bytes=24 * 1024 * 1024),
        cost_estimate=pl.CostEstimate(
            flops=0,
            bytes_accessed=4 * COST * sum(int(np.prod(s)) for s in out_shapes),
            transcendentals=0,
        ),
    )(*scalars, *arrays, *after)


class Plan:
    def __init__(self):
        found = plan()
        groups = batches(found)
        columns = []
        self.ways, self.slots, self.sources = {}, {}, {}

        def number_of(place, sources):
            if place not in sources:
                sources.append(place)
            return sources.index(place)

        def add(table):
            base = sum(c.shape[1] for c in columns)
            columns.append(table.reshape(CORES, -1))
            return base

        for step in range(1, len(SCHEDULE)):
            sources, numbers = self.sources.setdefault(step, []), []
            table = np.full((CORES, 2), -1, np.int32)
            for way in range(2):
                used = set()
                for core, owner in enumerate(SCHEDULE[step][way]):
                    if owner >= 0:
                        table[core, way] = number_of(found[core][owner], sources)
                        used.add(int(table[core, way]))
                numbers.append(tuple(sorted(used)))
            self.ways[step] = (tuple(numbers), add(table))

        held = np.full((CORES, CORES, 2), -1, np.int32)
        for batch, group in enumerate(groups):
            depth = max(len(owners) for owners in group)
            step = CHECKPOINTS[batch] + 2
            sources, numbers = self.sources.setdefault(step, []), [set() for _ in range(depth)]
            table = np.full((CORES, depth, 2), -1, np.int32)
            for core, owners in enumerate(group):
                for slot, owner in enumerate(owners):
                    held[core, owner] = (batch, slot)
                    table[core, slot] = owner, number_of(found[core][owner], sources)
                    numbers[slot].add(int(table[core, slot, 1]))
            self.slots[step] = (tuple(tuple(sorted(n)) for n in numbers), add(table))
        place = held.copy()
        for core in range(CORES):
            for owner in range(CORES):
                if held[core, owner, 0] < 0 <= held[core ^ 1, owner, 0]:
                    place[core, owner] = held[core ^ 1, owner]
                    place[core, owner, 0] += len(CHECKPOINTS)
        self.place = add(place)
        self.table = np.concatenate(columns, axis=1)


SWAP = [(i, i ^ 1) for i in range(CORES)]


def exchange(kv, selected, other_selected, index):
    tables = Plan()
    row = jnp.asarray(tables.table)[index]
    arrived = {"own": kv, "other": lax.ppermute(kv, "ctx", SWAP)}

    def pairs(step, way):
        return [(a, target(way, a)) for a, owner in enumerate(SCHEDULE[step][way]) if owner >= 0]

    choices = jnp.stack([selected.reshape(-1), other_selected.reshape(-1)])[:, None, :]
    owner = jnp.arange(CORES, dtype=jnp.int32)[None, :, None]
    named = (choices >= 0) & (choices // BLOCKS == owner)
    want = jnp.max(jnp.where(named, choices % BLOCKS, -1), axis=2).reshape(-1)

    kept, passed = [], []
    for step in range(CHECKPOINTS[-1] + 3):
        none = ((), 0)
        ways, slots = tables.ways.get(step, none), tables.slots.get(step, none)
        if step == 0:
            buffers = [kv, kv]
        elif ways[0] or slots[0]:
            buffers = move(
                ways,
                slots,
                [row, want],
                [arrived[key] for key in tables.sources[step]],
                kv.shape[1],
                after=buffers[:1] if ways[0] else passed,
            )
        else:
            continue
        if step < len(SCHEDULE):
            for way in range(2):
                arrived[step, way] = lax.ppermute(buffers[way], "ctx", pairs(step, way))
        if slots[0]:
            keep, give = buffers[-2:]
            kept.append(keep)
            passed.append(lax.ppermute(give, "ctx", SWAP))
    return kept + passed, row, tables.place


def attention_kernel(q_heads, sources, place, info, row_ref, q_ref, kv_ref, *refs):
    chosen, (o_ref, keys, values, sems) = refs[:sources], refs[sources:]
    step = pl.program_id(0)
    steps = pl.num_programs(0)
    here = lax.rem(step, 2)
    own_to = pl.ds((SLOTS - 1) * BLOCK_TOKENS, BLOCK_TOKENS)

    def pair(block_ref, to, buf, slot):
        return (
            pltpu.make_async_copy(
                block_ref.at[:, pl.ds(0, HEAD_SIZE)], keys.at[buf, to], sems.at[buf, slot, 0]
            ),
            pltpu.make_async_copy(
                block_ref.at[:, pl.ds(HEAD_SIZE, HEAD_SIZE)],
                values.at[buf, to, pl.ds(0, HEAD_SIZE)],
                sems.at[buf, slot, 1],
            ),
        )

    def own_rows(at):
        return kv_ref.at[pl.ds(pl.multiple_of(at * BLOCK_TOKENS, BLOCK_TOKENS), BLOCK_TOKENS)]

    def choice(at, slot):
        block = info[at * (SLOTS - 1) + slot]
        owner = jnp.maximum(block, 0) // BLOCKS
        return jnp.where(block < 0, -1, row_ref[place + 2 * owner]), row_ref[place + 2 * owner + 1]

    def start(at, buf):
        for copy in pair(own_rows(at), own_to, buf, SLOTS - 1):
            copy.start()
        for slot in range(SLOTS - 1):
            to = pl.ds(slot * BLOCK_TOKENS, BLOCK_TOKENS)
            array, block = choice(at, slot)
            for number in range(sources):

                @pl.when(array == number)
                def _():
                    for copy in pair(chosen[number].at[block], to, buf, slot):
                        copy.start()

    @pl.when(step == 0)
    def _():
        start(step, here)

    @pl.when(step + 1 < steps)
    def _():
        start(step + 1, 1 - here)

    values[here, :, pl.ds(HEAD_SIZE, HEAD_SIZE)] = jnp.ones(
        (SLOTS * BLOCK_TOKENS, HEAD_SIZE), jnp.bfloat16
    )
    for copy in pair(own_rows(step), own_to, here, SLOTS - 1):
        copy.wait()
    for slot in range(SLOTS - 1):
        to = pl.ds(slot * BLOCK_TOKENS, BLOCK_TOKENS)
        array, _ = choice(step, slot)

        @pl.when(array >= 0)
        def _():
            for copy in pair(own_rows(step), to, here, slot):
                copy.wait()

        @pl.when(array < 0)
        def _():
            first = keys[here, pl.ds((SLOTS - 1) * BLOCK_TOKENS, 16), :][0:1, :]
            keys[here, to, :] = jnp.broadcast_to(first, (BLOCK_TOKENS, HEAD_SIZE))
            values[here, to, :] = jnp.zeros((BLOCK_TOKENS, 2 * HEAD_SIZE), jnp.bfloat16)

    row = lax.broadcasted_iota(jnp.int32, (TILE, TILE), 0)
    col = lax.broadcasted_iota(jnp.int32, (TILE, TILE), 1)
    causal = row >= col
    dims = (((1,), (1,)), ((), ()))

    for head in range(q_heads):
        lanes = pl.ds(head * HEAD_SIZE, HEAD_SIZE)
        for tile in range(BLOCK_TOKENS // TILE):
            rows = pl.ds(tile * TILE, TILE)
            full = (SLOTS - 1) * BLOCK_TOKENS + tile * TILE
            query = q_ref[rows, lanes]
            far = lax.dot_general(
                query, keys[here, pl.ds(0, full), :], dims, preferred_element_type=jnp.float32
            )
            near = lax.dot_general(
                query, keys[here, pl.ds(full, TILE), :], dims, preferred_element_type=jnp.float32
            )
            near = jnp.where(causal, near, -1e30)
            highest = jnp.maximum(
                jnp.max(far, axis=1, keepdims=True), jnp.max(near, axis=1, keepdims=True)
            )
            far = jnp.exp2((far - highest) * EXP2_SCALE).astype(jnp.bfloat16)
            near = jnp.exp2((near - highest) * EXP2_SCALE).astype(jnp.bfloat16)
            total = jnp.dot(
                far, values[here, pl.ds(0, full), :], preferred_element_type=jnp.float32
            ) + jnp.dot(
                near, values[here, pl.ds(full, TILE), :], preferred_element_type=jnp.float32
            )
            o_ref[rows, lanes] = (total[:, :HEAD_SIZE] / total[:, HEAD_SIZE:]).astype(jnp.bfloat16)


def attention(queries, kv, chosen, info, row, place):
    rows, width = queries.shape
    blocks = rows // BLOCK_TOKENS
    keys = SLOTS * BLOCK_TOKENS
    return pl.pallas_call(
        functools.partial(attention_kernel, width // HEAD_SIZE, len(chosen), place),
        out_shape=jax.ShapeDtypeStruct((rows, width), jnp.bfloat16),
        grid_spec=pltpu.PrefetchScalarGridSpec(
            num_scalar_prefetch=2,
            grid=(blocks,),
            in_specs=[pl.BlockSpec((BLOCK_TOKENS, width), lambda i, *_: (i, 0))]
            + [pl.BlockSpec(memory_space=pltpu.HBM)] * (1 + len(chosen)),
            out_specs=pl.BlockSpec((BLOCK_TOKENS, width), lambda i, *_: (i, 0)),
            scratch_shapes=[
                pltpu.VMEM((2, keys, HEAD_SIZE), jnp.bfloat16),
                pltpu.VMEM((2, keys, 2 * HEAD_SIZE), jnp.bfloat16),
                pltpu.SemaphoreType.DMA((2, SLOTS, 2)),
            ],
        ),
        compiler_params=pltpu.CompilerParams(
            dimension_semantics=("arbitrary",), vmem_limit_bytes=48 * 1024 * 1024
        ),
        cost_estimate=pl.CostEstimate(
            flops=4 * rows * (width // HEAD_SIZE) * keys * HEAD_SIZE,
            bytes_accessed=4 * rows * width + 4 * blocks * keys * HEAD_SIZE,
            transcendentals=rows * (width // HEAD_SIZE) * keys,
        ),
    )(info, row, queries, kv, *chosen)


def project_kernel(parts, depth, core, a_ref, mine_ref, other_ref, o_ref):
    first = pl.ds(pl.multiple_of(core[0] * depth, depth), depth)
    second = pl.ds(pl.multiple_of((1 - core[0]) * depth, depth), depth)
    total = jnp.zeros(o_ref.shape[1:], jnp.float32)
    for part in range(parts):
        total += jnp.dot(a_ref[part, :, first], mine_ref[part], preferred_element_type=jnp.float32)
        total += jnp.dot(a_ref[part, :, second], other_ref[part], preferred_element_type=jnp.float32)
    o_ref[0] = total.astype(jnp.bfloat16)


def project(attended, mine, other, core):
    parts, rows, features = attended.shape
    depth = mine.shape[1]
    columns = mine.shape[2] // parts
    return pl.pallas_call(
        functools.partial(project_kernel, parts, depth),
        out_shape=jax.ShapeDtypeStruct((parts, rows, columns), jnp.bfloat16),
        grid_spec=pltpu.PrefetchScalarGridSpec(
            num_scalar_prefetch=1,
            grid=(parts,),
            in_specs=[
                pl.BlockSpec((parts, rows, features), lambda i, t: (0, 0, 0)),
                pl.BlockSpec((parts, depth, columns), lambda i, t: (0, 0, i)),
                pl.BlockSpec((parts, depth, columns), lambda i, t: (0, 0, i)),
            ],
            out_specs=pl.BlockSpec((1, rows, columns), lambda i, t: (i, 0, 0)),
        ),
        compiler_params=pltpu.CompilerParams(
            dimension_semantics=("arbitrary",), vmem_limit_bytes=32 * 1024 * 1024
        ),
        cost_estimate=pl.CostEstimate(
            flops=2 * parts * parts * rows * features * columns,
            bytes_accessed=2 * parts * parts * features * columns + 4 * parts * rows * features,
            transcendentals=0,
        ),
    )(core, attended, mine, other)


def gather_weight(out_weight, core):
    half = out_weight.shape[0] // 2
    mine = lax.dynamic_slice_in_dim(out_weight, core * half, half, 0)
    groups = [
        [((side ^ x_hi) * (CORES // 2) + rest) * 8 + x_hi * 4 + y for x_hi in range(2) for y in range(4)]
        for side in range(2)
        for rest in range(CORES // 2)
    ]
    return lax.all_gather(mine, ("ctx", "head"), axis=0, axis_index_groups=groups)


def per_device(queries, key_state_matrix, value_state_matrix, selected, out_weight):
    head_count = lax.axis_size("head")
    index = lax.axis_index("ctx")
    core = index % 2
    rows, width = queries.shape
    kv = jnp.concatenate([key_state_matrix, value_state_matrix], axis=1)
    other_selected = lax.ppermute(selected, "ctx", SWAP)
    mine = gather_weight(out_weight, core)
    chosen, row, place = exchange(kv, selected, other_selected, index)
    mine, chosen[-1] = lax.optimization_barrier((mine, chosen[-1]))
    other = lax.ppermute(mine, "ctx", SWAP)
    attended = attention(queries, kv, chosen, selected.reshape(-1), row, place)
    tokens = lax.all_to_all(
        attended.reshape(head_count, rows // head_count, width), "head", 0, 0, tiled=True
    )
    mixed = project(tokens, mine, other, core[None])
    return lax.all_to_all(mixed, "head", 0, 0, tiled=True).reshape(rows, -1)


def solution(mesh):
    return jax.shard_map(
        per_device,
        mesh=mesh,
        in_specs=(
            P("ctx", "head"),
            P("ctx", "head"),
            P("ctx", "head"),
            P("ctx", None),
            P("head", None),
        ),
        out_specs=P("ctx", "head"),
        check_vma=False,
    )
```

```python
import functools

import jax
import jax.numpy as jnp
import numpy as np
from jax import lax
from jax.experimental import pallas as pl
from jax.experimental.pallas import tpu as pltpu
from jax.sharding import PartitionSpec as P

HEAD_SIZE = 128
BLOCK_TOKENS = 512
TILE = 256
SLOTS = 4
BLOCKS = 4
ROWS = BLOCKS * BLOCK_TOKENS
RING = 8
CORES = 4 * RING
EXP2_SCALE = HEAD_SIZE ** (-0.5) * 1.4426950408889634

SCHEDULE = (
    (
        (
            0, 1, 2, 3, 4, -1, 6, -1, 8, -1, 10, -1, 12, -1, 14, -1,
            16, 17, 18, 19, 20, -1, 22, -1, 24, -1, 26, -1, 28, -1, -1, -1,
        ),
        (
            -1, 1, -1, 3, -1, 5, -1, 7, -1, 9, -1, 11, -1, 13, -1, 15,
            -1, -1, -1, -1, -1, -1, -1, -1, -1, -1, -1, -1, -1, -1, -1, -1,
        ),
    ),
    (
        (
            1, 0, 3, 2, 5, -1, 7, -1, 9, -1, 11, -1, 13, -1, 15, -1,
            17, 16, 19, 18, 21, -1, 23, -1, 25, -1, 27, -1, 29, -1, -1, -1,
        ),
        (
            -1, 0, -1, 2, -1, 4, -1, 6, -1, 8, -1, 10, -1, 12, -1, 14,
            -1, -1, -1, -1, -1, -1, -1, -1, -1, -1, -1, -1, -1, -1, -1, -1,
        ),
    ),
    (
        (
            -1, 3, 0, -1, 2, -1, 4, -1, 6, -1, 8, -1, 10, -1, -1, 1,
            -1, 1, 16, 3, 18, 5, 20, 7, 22, 9, 24, 11, 26, 13, -1, 15,
        ),
        (
            14, -1, 0, -1, 2, -1, 4, -1, 6, -1, 8, -1, 10, -1, 12, -1,
            -1, -1, -1, -1, -1, -1, -1, -1, -1, -1, -1, -1, -1, -1, -1, -1,
        ),
    ),
    (
        (
            -1, 2, 1, -1, 3, -1, 5, -1, 7, -1, 9, -1, 11, -1, -1, 0,
            -1, 18, 17, 2, 19, 4, 21, 6, 23, 8, 25, 10, 27, 12, -1, 14,
        ),
        (
            15, -1, 1, -1, 3, -1, 5, -1, 7, -1, 9, -1, 11, -1, 13, -1,
            -1, -1, -1, -1, -1, -1, -1, -1, -1, -1, -1, -1, -1, -1, -1, -1,
        ),
    ),
    (
        (
            -1, -1, -1, -1, 0, -1, 2, -1, 4, -1, 6, -1, 8, 1, -1, 3,
            14, 19, -1, 5, 16, 7, 18, 9, 20, 11, 22, 13, 24, 15, 12, 1,
        ),
        (
            -1, -1, -1, -1, 0, -1, 2, -1, 4, -1, 6, -1, 8, -1, 10, -1,
            -1, -1, -1, -1, -1, -1, -1, -1, -1, -1, -1, -1, -1, -1, -1, -1,
        ),
    ),
    (
        (
            -1, -1, -1, -1, 1, -1, 3, -1, 5, -1, 7, -1, 9, 0, -1, 2,
            15, 0, -1, 4, 17, 6, 19, 8, 21, 10, 23, 12, 25, 14, 13, 16,
        ),
        (
            -1, -1, -1, -1, 1, -1, 3, -1, 5, -1, 7, -1, -1, 0, 11, -1,
            -1, -1, -1, -1, -1, -1, -1, -1, -1, -1, -1, -1, -1, -1, -1, -1,
        ),
    ),
    (
        (
            -1, -1, -1, -1, -1, -1, 0, -1, 2, -1, 4, 1, 6, 3, -1, -1,
            12, 5, 14, 7, 0, 9, 16, 11, 18, 13, 20, 15, 22, 1, 10, 19,
        ),
        (
            -1, -1, -1, -1, -1, -1, -1, -1, 2, -1, 4, -1, -1, 3, 8, -1,
            -1, -1, -1, -1, -1, -1, -1, -1, -1, -1, -1, -1, -1, -1, -1, -1,
        ),
    ),
    (
        (
            -1, -1, -1, -1, -1, -1, -1, -1, -1, -1, 5, -1, 7, -1, -1, -1,
            13, 4, 15, 6, -1, 8, 17, 10, 5, 12, 21, 14, 23, 16, 11, 17,
        ),
        (
            -1, -1, -1, -1, -1, -1, 1, -1, 3, -1, -1, 0, 7, -1, 9, -1,
            -1, -1, -1, -1, -1, -1, -1, -1, -1, -1, -1, -1, -1, -1, -1, -1,
        ),
    ),
    (
        (
            -1, -1, -1, -1, -1, -1, -1, -1, -1, -1, -1, -1, 4, -1, -1, -1,
            10, 2, 12, 9, 14, 11, 0, 13, 2, 15, 18, -1, 20, 19, 8, 5,
        ),
        (
            -1, -1, -1, -1, -1, -1, -1, -1, -1, 1, -1, 3, 6, -1, -1, 3,
            -1, -1, -1, -1, -1, -1, -1, -1, -1, -1, -1, -1, -1, -1, -1, -1,
        ),
    ),
    (
        (
            -1, -1, -1, -1, -1, -1, -1, -1, -1, -1, -1, -1, 5, -1, -1, -1,
            -1, 6, -1, -1, -1, -1, -1, -1, 17, -1, 9, -1, 21, -1, -1, 4,
        ),
        (
            -1, -1, -1, -1, -1, -1, -1, -1, -1, -1, -1, -1, -1, 2, 7, -1,
            -1, -1, -1, -1, -1, -1, -1, -1, -1, -1, -1, -1, -1, -1, -1, -1,
        ),
    ),
)
CHECKPOINTS = (5, 7, 9)
COST = 12


def target(way, core):
    if way == 1:
        return core + CORES // 2
    side, place = divmod(core, CORES // 2)
    return side * (CORES // 2) + (place + (2 if core % 2 == 0 else -2)) % (CORES // 2)


def plan():
    found = [{core: "own", core ^ 1: "other"} for core in range(CORES)]
    for step, sends in enumerate(SCHEDULE):
        for way, row in enumerate(sends):
            for core, owner in enumerate(row):
                if owner >= 0:
                    found[target(way, core)].setdefault(owner, (step, way))
    return found


def batches(found):
    out = []
    for number, last in enumerate(CHECKPOINTS):
        first = -2 if number == 0 else CHECKPOINTS[number - 1]
        out.append(
            [
                [
                    owner
                    for owner, place in sorted(held.items())
                    if (owner // 2 < core // 2 or owner == core ^ 1)
                    and first < (-1 if isinstance(place, str) else place[0]) <= last
                ]
                for core, held in enumerate(found)
            ]
        )
    return out


def in_hbm(array):
    return pltpu.with_memory_space_constraint(array, pltpu.HBM)


def start_from(refs, numbers, source, first, rows, to, sem):
    for number in numbers:

        @pl.when(source == number)
        def _():
            at = pl.ds(pl.multiple_of(first, BLOCK_TOKENS), rows)
            pltpu.make_async_copy(refs[number].at[at], to, sem).start()


def wait_for(refs, source, rows, to, sem):
    @pl.when(source >= 0)
    def _():
        pltpu.make_async_copy(refs[0].at[pl.ds(0, rows)], to, sem).wait()


def move_kernel(ways, way_base, slots, slot_base, row, want, *refs):
    outs = len(ways) + (2 if slots else 0)
    ins, outs, sems = refs[: -outs - 1], refs[-outs - 1 : -1], refs[-1]

    def block_of(slot, which):
        owner = row[slot_base + 2 * slot]
        block = jnp.where(owner >= 0, want[which * CORES + jnp.maximum(owner, 0)], -1)
        source = jnp.where(block >= 0, row[slot_base + 2 * slot + 1], -1)
        return source, jnp.maximum(block, 0) * BLOCK_TOKENS

    jobs = [(numbers, row[way_base + i], 0, ROWS, outs[i]) for i, numbers in enumerate(ways)]
    for slot, numbers in enumerate(slots):
        for which in range(2):
            source, first = block_of(slot, which)
            jobs.append((numbers, source, first, BLOCK_TOKENS, outs[len(ways) + which].at[slot]))
    for i, (numbers, source, first, rows, to) in enumerate(jobs):
        start_from(ins, numbers, source, first, rows, to, sems.at[i])
    for i, (numbers, source, first, rows, to) in enumerate(jobs):
        wait_for(ins, source, rows, to, sems.at[i])


def move(ways, slots, scalars, arrays, width, after=()):
    out_shapes = [(ROWS, width)] * len(ways[0]) + [(len(slots[0]), BLOCK_TOKENS, width)] * (2 if slots[0] else 0)

    def whole(shape):
        return pl.BlockSpec(shape, lambda *_: (0,) * len(shape))

    return pl.pallas_call(
        functools.partial(move_kernel, *ways, *slots),
        out_shape=[
            pltpu.HBM(s, arrays[0].dtype) if len(s) == 3 else jax.ShapeDtypeStruct(s, arrays[0].dtype)
            for s in out_shapes
        ],
        grid_spec=pltpu.PrefetchScalarGridSpec(
            num_scalar_prefetch=len(scalars),
            grid=(1,),
            in_specs=[pl.BlockSpec(memory_space=pltpu.HBM)] * (len(arrays) + len(after)),
            out_specs=[whole(s) for s in out_shapes],
            scratch_shapes=[pltpu.SemaphoreType.DMA((len(ways[0]) + 2 * len(slots[0]),))],
        ),
        compiler_params=pltpu.CompilerParams(vmem_limit_bytes=24 * 1024 * 1024),
        cost_estimate=pl.CostEstimate(
            flops=0,
            bytes_accessed=4 * COST * sum(int(np.prod(s)) for s in out_shapes),
            transcendentals=0,
        ),
    )(*scalars, *arrays, *after)


class Plan:
    def __init__(self):
        found = plan()
        groups = batches(found)
        columns = []
        self.ways, self.slots, self.sources = {}, {}, {}

        def number_of(place, sources):
            if place not in sources:
                sources.append(place)
            return sources.index(place)

        def add(table):
            base = sum(c.shape[1] for c in columns)
            columns.append(table.reshape(CORES, -1))
            return base

        for step in range(1, len(SCHEDULE)):
            sources, numbers = self.sources.setdefault(step, []), []
            table = np.full((CORES, 2), -1, np.int32)
            for way in range(2):
                used = set()
                for core, owner in enumerate(SCHEDULE[step][way]):
                    if owner >= 0:
                        table[core, way] = number_of(found[core][owner], sources)
                        used.add(int(table[core, way]))
                numbers.append(tuple(sorted(used)))
            self.ways[step] = (tuple(numbers), add(table))

        held = np.full((CORES, CORES, 2), -1, np.int32)
        for batch, group in enumerate(groups):
            depth = max(len(owners) for owners in group)
            step = CHECKPOINTS[batch] + 2
            sources, numbers = self.sources.setdefault(step, []), [set() for _ in range(depth)]
            table = np.full((CORES, depth, 2), -1, np.int32)
            for core, owners in enumerate(group):
                for slot, owner in enumerate(owners):
                    held[core, owner] = (batch, slot)
                    table[core, slot] = owner, number_of(found[core][owner], sources)
                    numbers[slot].add(int(table[core, slot, 1]))
            self.slots[step] = (tuple(tuple(sorted(n)) for n in numbers), add(table))
        place = held.copy()
        for core in range(CORES):
            for owner in range(CORES):
                if held[core, owner, 0] < 0 <= held[core ^ 1, owner, 0]:
                    place[core, owner] = held[core ^ 1, owner]
                    place[core, owner, 0] += len(CHECKPOINTS)
        self.place = add(place)
        self.table = np.concatenate(columns, axis=1)


SWAP = [(i, i ^ 1) for i in range(CORES)]


def exchange(kv, selected, other_selected, index):
    tables = Plan()
    row = jnp.asarray(tables.table)[index]
    arrived = {"own": kv, "other": lax.ppermute(kv, "ctx", SWAP)}

    def pairs(step, way):
        return [(a, target(way, a)) for a, owner in enumerate(SCHEDULE[step][way]) if owner >= 0]

    choices = jnp.stack([selected.reshape(-1), other_selected.reshape(-1)])[:, None, :]
    owner = jnp.arange(CORES, dtype=jnp.int32)[None, :, None]
    named = (choices >= 0) & (choices // BLOCKS == owner)
    want = jnp.max(jnp.where(named, choices % BLOCKS, -1), axis=2).reshape(-1)

    kept, passed = [], []
    for step in range(CHECKPOINTS[-1] + 3):
        none = ((), 0)
        ways, slots = tables.ways.get(step, none), tables.slots.get(step, none)
        if step == 0:
            buffers = [kv, kv]
        elif ways[0] or slots[0]:
            buffers = move(
                ways,
                slots,
                [row, want],
                [arrived[key] for key in tables.sources[step]],
                kv.shape[1],
                after=buffers[:1] if ways[0] else passed,
            )
        else:
            continue
        if step < len(SCHEDULE):
            for way in range(2):
                arrived[step, way] = lax.ppermute(buffers[way], "ctx", pairs(step, way))
        if slots[0]:
            keep, give = buffers[-2:]
            kept.append(keep)
            passed.append(lax.ppermute(give, "ctx", SWAP))
    return kept + passed, row, tables.place


def attention_kernel(q_heads, sources, place, info, row_ref, q_ref, kv_ref, *refs):
    chosen, (o_ref, keys, values, sems) = refs[:sources], refs[sources:]
    step = pl.program_id(0)
    steps = pl.num_programs(0)
    here = lax.rem(step, 2)
    own_to = pl.ds((SLOTS - 1) * BLOCK_TOKENS, BLOCK_TOKENS)

    def pair(block_ref, to, buf, slot):
        return (
            pltpu.make_async_copy(
                block_ref.at[:, pl.ds(0, HEAD_SIZE)], keys.at[buf, to], sems.at[buf, slot, 0]
            ),
            pltpu.make_async_copy(
                block_ref.at[:, pl.ds(HEAD_SIZE, HEAD_SIZE)],
                values.at[buf, to, pl.ds(0, HEAD_SIZE)],
                sems.at[buf, slot, 1],
            ),
        )

    def own_rows(at):
        return kv_ref.at[pl.ds(pl.multiple_of(at * BLOCK_TOKENS, BLOCK_TOKENS), BLOCK_TOKENS)]

    def choice(at, slot):
        block = info[at * (SLOTS - 1) + slot]
        owner = jnp.maximum(block, 0) // BLOCKS
        return jnp.where(block < 0, -1, row_ref[place + 2 * owner]), row_ref[place + 2 * owner + 1]

    def start(at, buf):
        for copy in pair(own_rows(at), own_to, buf, SLOTS - 1):
            copy.start()
        for slot in range(SLOTS - 1):
            to = pl.ds(slot * BLOCK_TOKENS, BLOCK_TOKENS)
            array, block = choice(at, slot)
            for number in range(sources):

                @pl.when(array == number)
                def _():
                    for copy in pair(chosen[number].at[block], to, buf, slot):
                        copy.start()

    @pl.when(step == 0)
    def _():
        start(step, here)

    @pl.when(step + 1 < steps)
    def _():
        start(step + 1, 1 - here)

    values[here, :, pl.ds(HEAD_SIZE, HEAD_SIZE)] = jnp.ones(
        (SLOTS * BLOCK_TOKENS, HEAD_SIZE), jnp.bfloat16
    )
    for copy in pair(own_rows(step), own_to, here, SLOTS - 1):
        copy.wait()
    for slot in range(SLOTS - 1):
        to = pl.ds(slot * BLOCK_TOKENS, BLOCK_TOKENS)
        array, _ = choice(step, slot)

        @pl.when(array >= 0)
        def _():
            for copy in pair(own_rows(step), to, here, slot):
                copy.wait()

        @pl.when(array < 0)
        def _():
            first = keys[here, pl.ds((SLOTS - 1) * BLOCK_TOKENS, 16), :][0:1, :]
            keys[here, to, :] = jnp.broadcast_to(first, (BLOCK_TOKENS, HEAD_SIZE))
            values[here, to, :] = jnp.zeros((BLOCK_TOKENS, 2 * HEAD_SIZE), jnp.bfloat16)

    row = lax.broadcasted_iota(jnp.int32, (TILE, TILE), 0)
    col = lax.broadcasted_iota(jnp.int32, (TILE, TILE), 1)
    causal = row >= col
    dims = (((1,), (1,)), ((), ()))

    units = [(head, tile) for head in range(q_heads) for tile in range(BLOCK_TOKENS // TILE)]

    def places(unit):
        head, tile = unit
        far = (SLOTS - 1) * BLOCK_TOKENS + tile * TILE
        return pl.ds(tile * TILE, TILE), pl.ds(head * HEAD_SIZE, HEAD_SIZE), pl.ds(0, far), pl.ds(far, TILE)

    def scores(unit):
        rows, lanes, *parts = places(unit)
        query = q_ref[rows, lanes]
        far, near = (
            lax.dot_general(query, keys[here, at, :], dims, preferred_element_type=jnp.float32)
            for at in parts
        )
        return far, jnp.where(causal, near, -1e30)

    following = scores(units[0])
    for number, unit in enumerate(units):
        now = following
        if number + 1 < len(units):
            following = scores(units[number + 1])
        rows, lanes, *parts = places(unit)
        highest = functools.reduce(jnp.maximum, [jnp.max(s, axis=1, keepdims=True) for s in now])
        total = sum(
            jnp.dot(
                jnp.exp2((s - highest) * EXP2_SCALE).astype(jnp.bfloat16),
                values[here, at, :],
                preferred_element_type=jnp.float32,
            )
            for s, at in zip(now, parts)
        )
        o_ref[rows, lanes] = (total[:, :HEAD_SIZE] / total[:, HEAD_SIZE:]).astype(jnp.bfloat16)


def attention(queries, kv, chosen, info, row, place):
    rows, width = queries.shape
    blocks = rows // BLOCK_TOKENS
    keys = SLOTS * BLOCK_TOKENS
    return pl.pallas_call(
        functools.partial(attention_kernel, width // HEAD_SIZE, len(chosen), place),
        out_shape=jax.ShapeDtypeStruct((rows, width), jnp.bfloat16),
        grid_spec=pltpu.PrefetchScalarGridSpec(
            num_scalar_prefetch=2,
            grid=(blocks,),
            in_specs=[pl.BlockSpec((BLOCK_TOKENS, width), lambda i, *_: (i, 0))]
            + [pl.BlockSpec(memory_space=pltpu.HBM)] * (1 + len(chosen)),
            out_specs=pl.BlockSpec((BLOCK_TOKENS, width), lambda i, *_: (i, 0)),
            scratch_shapes=[
                pltpu.VMEM((2, keys, HEAD_SIZE), jnp.bfloat16),
                pltpu.VMEM((2, keys, 2 * HEAD_SIZE), jnp.bfloat16),
                pltpu.SemaphoreType.DMA((2, SLOTS, 2)),
            ],
        ),
        compiler_params=pltpu.CompilerParams(
            dimension_semantics=("arbitrary",), vmem_limit_bytes=48 * 1024 * 1024
        ),
        cost_estimate=pl.CostEstimate(
            flops=4 * rows * (width // HEAD_SIZE) * keys * HEAD_SIZE,
            bytes_accessed=4 * rows * width + 4 * blocks * keys * HEAD_SIZE,
            transcendentals=rows * (width // HEAD_SIZE) * keys,
        ),
    )(info, row, *map(in_hbm, (queries, kv, *chosen)))


def project_kernel(depth, core, a_ref, mine_ref, other_ref, o_ref, first, second):
    parts, rows, _ = a_ref.shape

    @pl.when(pl.program_id(0) == 0)
    def _():
        for to, half in ((first, core[0]), (second, 1 - core[0])):
            lanes = pl.ds(pl.multiple_of(half * depth, depth), depth)
            for part in range(parts):
                to[:, pl.ds(part * depth, depth)] = a_ref[part, :, lanes]

    columns = o_ref.shape[2]
    for number in range(o_ref.shape[0]):
        at = pl.ds(number * columns, columns)
        total = sum(
            jnp.dot(
                a[...], w[:, :, at].reshape(parts * depth, columns), preferred_element_type=jnp.float32
            )
            for a, w in ((first, mine_ref), (second, other_ref))
        )
        o_ref[number] = total.astype(jnp.bfloat16)


def project(attended, mine, other, core):
    parts, rows, features = attended.shape
    depth = mine.shape[1]
    columns = mine.shape[2] // parts
    together = 2
    return pl.pallas_call(
        functools.partial(project_kernel, depth),
        out_shape=jax.ShapeDtypeStruct((parts, rows, columns), jnp.bfloat16),
        grid_spec=pltpu.PrefetchScalarGridSpec(
            num_scalar_prefetch=1,
            grid=(parts // together,),
            in_specs=[
                pl.BlockSpec((parts, rows, features), lambda i, t: (0, 0, 0)),
                pl.BlockSpec((parts, depth, together * columns), lambda i, t: (0, 0, i)),
                pl.BlockSpec((parts, depth, together * columns), lambda i, t: (0, 0, i)),
            ],
            out_specs=pl.BlockSpec((together, rows, columns), lambda i, t: (i, 0, 0)),
            scratch_shapes=[pltpu.VMEM((rows, parts * depth), jnp.bfloat16)] * 2,
        ),
        compiler_params=pltpu.CompilerParams(
            dimension_semantics=("arbitrary",), vmem_limit_bytes=32 * 1024 * 1024
        ),
        cost_estimate=pl.CostEstimate(
            flops=2 * parts * parts * rows * features * columns,
            bytes_accessed=2 * parts * parts * features * columns + 4 * parts * rows * features,
            transcendentals=0,
        ),
    )(core, attended, in_hbm(mine), in_hbm(other))


def gather_weight(out_weight, core):
    half = out_weight.shape[0] // 2
    mine = lax.dynamic_slice_in_dim(out_weight, core * half, half, 0)
    groups = [
        [((side ^ x_hi) * (CORES // 2) + rest) * 8 + x_hi * 4 + y for x_hi in range(2) for y in range(4)]
        for side in range(2)
        for rest in range(CORES // 2)
    ]
    return lax.all_gather(mine, ("ctx", "head"), axis=0, axis_index_groups=groups)


def per_device(queries, key_state_matrix, value_state_matrix, selected, out_weight):
    head_count = lax.axis_size("head")
    index = lax.axis_index("ctx")
    core = index % 2
    rows, width = queries.shape
    kv = jnp.concatenate([key_state_matrix, value_state_matrix], axis=1)
    other_selected = lax.ppermute(selected, "ctx", SWAP)
    mine = gather_weight(out_weight, core)
    chosen, row, place = exchange(kv, selected, other_selected, index)
    mine, chosen[-1] = lax.optimization_barrier((mine, chosen[-1]))
    other = lax.ppermute(mine, "ctx", SWAP)
    attended = attention(queries, kv, chosen, selected.reshape(-1), row, place)
    tokens = lax.all_to_all(
        attended.reshape(head_count, rows // head_count, width), "head", 0, 0, tiled=True
    )
    mixed = project(tokens, mine, other, core[None])
    return lax.all_to_all(mixed, "head", 0, 0, tiled=True).reshape(rows, -1)


def solution(mesh):
    return jax.shard_map(
        per_device,
        mesh=mesh,
        in_specs=(
            P("ctx", "head"),
            P("ctx", "head"),
            P("ctx", "head"),
            P("ctx", None),
            P("head", None),
        ),
        out_specs=P("ctx", "head"),
        check_vma=False,
    )
```

```python
import functools

import jax
import jax.numpy as jnp
import numpy as np
from jax import lax
from jax.experimental import pallas as pl
from jax.experimental.pallas import tpu as pltpu
from jax.sharding import PartitionSpec as P

HEAD_SIZE = 128
BLOCK_TOKENS = 512
TILE = 256
SLOTS = 4
BLOCKS = 4
ROWS = BLOCKS * BLOCK_TOKENS
RING = 8
CORES = 4 * RING
EXP2_SCALE = HEAD_SIZE ** (-0.5) * 1.4426950408889634

SCHEDULE = (
    (
        (
            0, 1, 2, 3, 4, -1, 6, -1, 8, -1, 10, -1, 12, -1, 14, -1,
            16, 17, 18, 19, 20, -1, 22, -1, 24, -1, 26, -1, 28, -1, -1, -1,
        ),
        (
            -1, 1, -1, 3, -1, 5, -1, 7, -1, 9, -1, 11, -1, 13, -1, 15,
            -1, -1, -1, -1, -1, -1, -1, -1, -1, -1, -1, -1, -1, -1, -1, -1,
        ),
    ),
    (
        (
            1, 0, 3, 2, 5, -1, 7, -1, 9, -1, 11, -1, 13, -1, 15, -1,
            17, 16, 19, 18, 21, -1, 23, -1, 25, -1, 27, -1, 29, -1, -1, -1,
        ),
        (
            -1, 0, -1, 2, -1, 4, -1, 6, -1, 8, -1, 10, -1, 12, -1, 14,
            -1, -1, -1, -1, -1, -1, -1, -1, -1, -1, -1, -1, -1, -1, -1, -1,
        ),
    ),
    (
        (
            -1, 3, 0, -1, 2, -1, 4, -1, 6, -1, 8, -1, 10, -1, -1, 1,
            -1, 1, 16, 3, 18, 5, 20, 7, 22, 9, 24, 11, 26, 13, -1, 15,
        ),
        (
            14, -1, 0, -1, 2, -1, 4, -1, 6, -1, 8, -1, 10, -1, 12, -1,
            -1, -1, -1, -1, -1, -1, -1, -1, -1, -1, -1, -1, -1, -1, -1, -1,
        ),
    ),
    (
        (
            -1, 2, 1, -1, 3, -1, 5, -1, 7, -1, 9, -1, 11, -1, -1, 0,
            -1, 18, 17, 2, 19, 4, 21, 6, 23, 8, 25, 10, 27, 12, -1, 14,
        ),
        (
            15, -1, 1, -1, 3, -1, 5, -1, 7, -1, 9, -1, 11, -1, 13, -1,
            -1, -1, -1, -1, -1, -1, -1, -1, -1, -1, -1, -1, -1, -1, -1, -1,
        ),
    ),
    (
        (
            -1, -1, -1, -1, 0, -1, 2, -1, 4, -1, 6, -1, 8, 1, -1, 3,
            14, 19, -1, 5, 16, 7, 18, 9, 20, 11, 22, 13, 24, 15, 12, 1,
        ),
        (
            -1, -1, -1, -1, 0, -1, 2, -1, 4, -1, 6, -1, 8, -1, 10, -1,
            -1, -1, -1, -1, -1, -1, -1, -1, -1, -1, -1, -1, -1, -1, -1, -1,
        ),
    ),
    (
        (
            -1, -1, -1, -1, 1, -1, 3, -1, 5, -1, 7, -1, 9, 0, -1, 2,
            15, 0, -1, 4, 17, 6, 19, 8, 21, 10, 23, 12, 25, 14, 13, 16,
        ),
        (
            -1, -1, -1, -1, 1, -1, 3, -1, 5, -1, 7, -1, -1, 0, 11, -1,
            -1, -1, -1, -1, -1, -1, -1, -1, -1, -1, -1, -1, -1, -1, -1, -1,
        ),
    ),
    (
        (
            -1, -1, -1, -1, -1, -1, 0, -1, 2, -1, 4, 1, 6, 3, -1, -1,
            12, 5, 14, 7, 0, 9, 16, 11, 18, 13, 20, 15, 22, 1, 10, 19,
        ),
        (
            -1, -1, -1, -1, -1, -1, -1, -1, 2, -1, 4, -1, -1, 3, 8, -1,
            -1, -1, -1, -1, -1, -1, -1, -1, -1, -1, -1, -1, -1, -1, -1, -1,
        ),
    ),
    (
        (
            -1, -1, -1, -1, -1, -1, -1, -1, -1, -1, 5, -1, 7, -1, -1, -1,
            13, 4, 15, 6, -1, 8, 17, 10, 5, 12, 21, 14, 23, 16, 11, 17,
        ),
        (
            -1, -1, -1, -1, -1, -1, 1, -1, 3, -1, -1, 0, 7, -1, 9, -1,
            -1, -1, -1, -1, -1, -1, -1, -1, -1, -1, -1, -1, -1, -1, -1, -1,
        ),
    ),
    (
        (
            -1, -1, -1, -1, -1, -1, -1, -1, -1, -1, -1, -1, 4, -1, -1, -1,
            10, 2, 12, 9, 14, 11, 0, 13, 2, 15, 18, -1, 20, 19, 8, 5,
        ),
        (
            -1, -1, -1, -1, -1, -1, -1, -1, -1, 1, -1, 3, 6, -1, -1, 3,
            -1, -1, -1, -1, -1, -1, -1, -1, -1, -1, -1, -1, -1, -1, -1, -1,
        ),
    ),
    (
        (
            -1, -1, -1, -1, -1, -1, -1, -1, -1, -1, -1, -1, 5, -1, -1, -1,
            -1, 6, -1, -1, -1, -1, -1, -1, 17, -1, 9, -1, 21, -1, -1, 4,
        ),
        (
            -1, -1, -1, -1, -1, -1, -1, -1, -1, -1, -1, -1, -1, 2, 7, -1,
            -1, -1, -1, -1, -1, -1, -1, -1, -1, -1, -1, -1, -1, -1, -1, -1,
        ),
    ),
)
CHECKPOINTS = (5, 7, 9)
CHUNKS = 2
COST = 12


def target(way, core):
    if way == 1:
        return core + CORES // 2
    side, place = divmod(core, CORES // 2)
    return side * (CORES // 2) + (place + (2 if core % 2 == 0 else -2)) % (CORES // 2)


def plan():
    found = [{core: "own", core ^ 1: "other"} for core in range(CORES)]
    for step, sends in enumerate(SCHEDULE):
        for way, row in enumerate(sends):
            for core, owner in enumerate(row):
                if owner >= 0:
                    found[target(way, core)].setdefault(owner, (step, way))
    return found


def batches(found):
    out = []
    for number, last in enumerate(CHECKPOINTS):
        first = -2 if number == 0 else CHECKPOINTS[number - 1]
        out.append(
            [
                [
                    owner
                    for owner, place in sorted(held.items())
                    if (owner // 2 < core // 2 or owner == core ^ 1)
                    and first < (-1 if isinstance(place, str) else place[0]) <= last
                ]
                for core, held in enumerate(found)
            ]
        )
    return out


def in_hbm(array):
    return pltpu.with_memory_space_constraint(array, pltpu.HBM)


def start_from(refs, numbers, source, first, rows, to, sem):
    for number in numbers:

        @pl.when(source == number)
        def _():
            at = pl.ds(pl.multiple_of(first, BLOCK_TOKENS), rows)
            pltpu.make_async_copy(refs[number].at[at], to, sem).start()


def wait_for(refs, source, rows, to, sem):
    @pl.when(source >= 0)
    def _():
        pltpu.make_async_copy(refs[0].at[pl.ds(0, rows)], to, sem).wait()


def move_kernel(ways, way_base, slots, slot_base, row, want, *refs):
    outs = len(ways) + (2 if slots else 0)
    ins, outs, sems = refs[: -outs - 1], refs[-outs - 1 : -1], refs[-1]

    def block_of(slot, which):
        owner = row[slot_base + 2 * slot]
        block = jnp.where(owner >= 0, want[which * CORES + jnp.maximum(owner, 0)], -1)
        source = jnp.where(block >= 0, row[slot_base + 2 * slot + 1], -1)
        return source, jnp.maximum(block, 0) * BLOCK_TOKENS

    jobs = [(numbers, row[way_base + i], 0, ROWS, outs[i]) for i, numbers in enumerate(ways)]
    for slot, numbers in enumerate(slots):
        for which in range(2):
            source, first = block_of(slot, which)
            jobs.append((numbers, source, first, BLOCK_TOKENS, outs[len(ways) + which].at[slot]))
    for i, (numbers, source, first, rows, to) in enumerate(jobs):
        start_from(ins, numbers, source, first, rows, to, sems.at[i])
    for i, (numbers, source, first, rows, to) in enumerate(jobs):
        wait_for(ins, source, rows, to, sems.at[i])


def move(ways, slots, scalars, arrays, width, after=()):
    out_shapes = [(ROWS, width)] * len(ways[0]) + [(len(slots[0]), BLOCK_TOKENS, width)] * (2 if slots[0] else 0)

    def whole(shape):
        return pl.BlockSpec(shape, lambda *_: (0,) * len(shape))

    return pl.pallas_call(
        functools.partial(move_kernel, *ways, *slots),
        out_shape=[
            pltpu.HBM(s, arrays[0].dtype) if len(s) == 3 else jax.ShapeDtypeStruct(s, arrays[0].dtype)
            for s in out_shapes
        ],
        grid_spec=pltpu.PrefetchScalarGridSpec(
            num_scalar_prefetch=len(scalars),
            grid=(1,),
            in_specs=[pl.BlockSpec(memory_space=pltpu.HBM)] * (len(arrays) + len(after)),
            out_specs=[whole(s) for s in out_shapes],
            scratch_shapes=[pltpu.SemaphoreType.DMA((len(ways[0]) + 2 * len(slots[0]),))],
        ),
        compiler_params=pltpu.CompilerParams(vmem_limit_bytes=24 * 1024 * 1024),
        cost_estimate=pl.CostEstimate(
            flops=0,
            bytes_accessed=4 * COST * sum(int(np.prod(s)) for s in out_shapes),
            transcendentals=0,
        ),
    )(*scalars, *arrays, *after)


class Plan:
    def __init__(self):
        found = plan()
        groups = batches(found)
        columns = []
        self.ways, self.slots, self.sources = {}, {}, {}

        def number_of(place, sources):
            if place not in sources:
                sources.append(place)
            return sources.index(place)

        def add(table):
            base = sum(c.shape[1] for c in columns)
            columns.append(table.reshape(CORES, -1))
            return base

        for step in range(1, len(SCHEDULE)):
            sources, numbers = self.sources.setdefault(step, []), []
            table = np.full((CORES, 2), -1, np.int32)
            for way in range(2):
                used = set()
                for core, owner in enumerate(SCHEDULE[step][way]):
                    if owner >= 0:
                        table[core, way] = number_of(found[core][owner], sources)
                        used.add(int(table[core, way]))
                numbers.append(tuple(sorted(used)))
            self.ways[step] = (tuple(numbers), add(table))

        held = np.full((CORES, CORES, 2), -1, np.int32)
        for batch, group in enumerate(groups):
            depth = max(len(owners) for owners in group)
            step = CHECKPOINTS[batch] + 2
            sources, numbers = self.sources.setdefault(step, []), [set() for _ in range(depth)]
            table = np.full((CORES, depth, 2), -1, np.int32)
            for core, owners in enumerate(group):
                for slot, owner in enumerate(owners):
                    held[core, owner] = (batch, slot)
                    table[core, slot] = owner, number_of(found[core][owner], sources)
                    numbers[slot].add(int(table[core, slot, 1]))
            self.slots[step] = (tuple(tuple(sorted(n)) for n in numbers), add(table))
        place = held.copy()
        for core in range(CORES):
            for owner in range(CORES):
                if held[core, owner, 0] < 0 <= held[core ^ 1, owner, 0]:
                    place[core, owner] = held[core ^ 1, owner]
                    place[core, owner, 0] += len(CHECKPOINTS)
        self.place = add(place)
        self.table = np.concatenate(columns, axis=1)


SWAP = [(i, i ^ 1) for i in range(CORES)]


def exchange(kv, selected, other_selected, index):
    tables = Plan()
    row = jnp.asarray(tables.table)[index]
    arrived = {"own": kv, "other": lax.ppermute(kv, "ctx", SWAP)}

    def pairs(step, way):
        return [(a, target(way, a)) for a, owner in enumerate(SCHEDULE[step][way]) if owner >= 0]

    choices = jnp.stack([selected.reshape(-1), other_selected.reshape(-1)])[:, None, :]
    owner = jnp.arange(CORES, dtype=jnp.int32)[None, :, None]
    named = (choices >= 0) & (choices // BLOCKS == owner)
    want = jnp.max(jnp.where(named, choices % BLOCKS, -1), axis=2).reshape(-1)

    kept, passed = [], []
    for step in range(CHECKPOINTS[-1] + 3):
        none = ((), 0)
        ways, slots = tables.ways.get(step, none), tables.slots.get(step, none)
        if step == 0:
            buffers = [kv, kv]
        elif ways[0] or slots[0]:
            buffers = move(
                ways,
                slots,
                [row, want],
                [arrived[key] for key in tables.sources[step]],
                kv.shape[1],
                after=buffers[:1] if ways[0] else passed,
            )
        else:
            continue
        if step < len(SCHEDULE):
            for way in range(2):
                arrived[step, way] = lax.ppermute(buffers[way], "ctx", pairs(step, way))
        if slots[0]:
            keep, give = buffers[-2:]
            kept.append(keep)
            passed.append(lax.ppermute(give, "ctx", SWAP))
    return kept + passed, row, tables.place


def attention_kernel(q_heads, sources, place, first, info, row_ref, q_ref, kv_ref, *refs):
    chosen, (o_ref, keys, values, sems) = refs[:sources], refs[sources:]
    step = pl.program_id(0)
    steps = pl.num_programs(0)
    here = lax.rem(step, 2)
    own_to = pl.ds((SLOTS - 1) * BLOCK_TOKENS, BLOCK_TOKENS)

    def pair(block_ref, to, buf, slot):
        return (
            pltpu.make_async_copy(
                block_ref.at[:, pl.ds(0, HEAD_SIZE)], keys.at[buf, to], sems.at[buf, slot, 0]
            ),
            pltpu.make_async_copy(
                block_ref.at[:, pl.ds(HEAD_SIZE, HEAD_SIZE)],
                values.at[buf, to, pl.ds(0, HEAD_SIZE)],
                sems.at[buf, slot, 1],
            ),
        )

    def own_rows(at):
        return kv_ref.at[pl.ds(pl.multiple_of((first + at) * BLOCK_TOKENS, BLOCK_TOKENS), BLOCK_TOKENS)]

    def choice(at, slot):
        block = info[(first + at) * (SLOTS - 1) + slot]
        owner = jnp.maximum(block, 0) // BLOCKS
        return jnp.where(block < 0, -1, row_ref[place + 2 * owner]), row_ref[place + 2 * owner + 1]

    def start(at, buf):
        for copy in pair(own_rows(at), own_to, buf, SLOTS - 1):
            copy.start()
        for slot in range(SLOTS - 1):
            to = pl.ds(slot * BLOCK_TOKENS, BLOCK_TOKENS)
            array, block = choice(at, slot)
            for number in range(sources):

                @pl.when(array == number)
                def _():
                    for copy in pair(chosen[number].at[block], to, buf, slot):
                        copy.start()

    @pl.when(step == 0)
    def _():
        start(step, here)

    @pl.when(step + 1 < steps)
    def _():
        start(step + 1, 1 - here)

    values[here, :, pl.ds(HEAD_SIZE, HEAD_SIZE)] = jnp.ones(
        (SLOTS * BLOCK_TOKENS, HEAD_SIZE), jnp.bfloat16
    )
    for copy in pair(own_rows(step), own_to, here, SLOTS - 1):
        copy.wait()
    for slot in range(SLOTS - 1):
        to = pl.ds(slot * BLOCK_TOKENS, BLOCK_TOKENS)
        array, _ = choice(step, slot)

        @pl.when(array >= 0)
        def _():
            for copy in pair(own_rows(step), to, here, slot):
                copy.wait()

        @pl.when(array < 0)
        def _():
            first = keys[here, pl.ds((SLOTS - 1) * BLOCK_TOKENS, 16), :][0:1, :]
            keys[here, to, :] = jnp.broadcast_to(first, (BLOCK_TOKENS, HEAD_SIZE))
            values[here, to, :] = jnp.zeros((BLOCK_TOKENS, 2 * HEAD_SIZE), jnp.bfloat16)

    row = lax.broadcasted_iota(jnp.int32, (TILE, TILE), 0)
    col = lax.broadcasted_iota(jnp.int32, (TILE, TILE), 1)
    causal = row >= col
    dims = (((1,), (1,)), ((), ()))

    units = [(head, tile) for head in range(q_heads) for tile in range(BLOCK_TOKENS // TILE)]

    def places(unit):
        head, tile = unit
        far = (SLOTS - 1) * BLOCK_TOKENS + tile * TILE
        return pl.ds(tile * TILE, TILE), pl.ds(head * HEAD_SIZE, HEAD_SIZE), pl.ds(0, far), pl.ds(far, TILE)

    def scores(unit):
        rows, lanes, *parts = places(unit)
        query = q_ref[rows, lanes]
        far, near = (
            lax.dot_general(query, keys[here, at, :], dims, preferred_element_type=jnp.float32)
            for at in parts
        )
        return far, jnp.where(causal, near, -1e30)

    following = scores(units[0])
    for number, unit in enumerate(units):
        now = following
        if number + 1 < len(units):
            following = scores(units[number + 1])
        rows, lanes, *parts = places(unit)
        highest = functools.reduce(jnp.maximum, [jnp.max(s, axis=1, keepdims=True) for s in now])
        total = sum(
            jnp.dot(
                jnp.exp2((s - highest) * EXP2_SCALE).astype(jnp.bfloat16),
                values[here, at, :],
                preferred_element_type=jnp.float32,
            )
            for s, at in zip(now, parts)
        )
        o_ref[rows, lanes] = (total[:, :HEAD_SIZE] / total[:, HEAD_SIZE:]).astype(jnp.bfloat16)


def attention(queries, kv, chosen, info, row, place, first, blocks):
    width = queries.shape[1]
    rows = blocks * BLOCK_TOKENS
    keys = SLOTS * BLOCK_TOKENS
    return pl.pallas_call(
        functools.partial(attention_kernel, width // HEAD_SIZE, len(chosen), place, first),
        out_shape=jax.ShapeDtypeStruct((rows, width), jnp.bfloat16),
        grid_spec=pltpu.PrefetchScalarGridSpec(
            num_scalar_prefetch=2,
            grid=(blocks,),
            in_specs=[pl.BlockSpec((BLOCK_TOKENS, width), lambda i, *_: (first + i, 0))]
            + [pl.BlockSpec(memory_space=pltpu.HBM)] * (1 + len(chosen)),
            out_specs=pl.BlockSpec((BLOCK_TOKENS, width), lambda i, *_: (i, 0)),
            scratch_shapes=[
                pltpu.VMEM((2, keys, HEAD_SIZE), jnp.bfloat16),
                pltpu.VMEM((2, keys, 2 * HEAD_SIZE), jnp.bfloat16),
                pltpu.SemaphoreType.DMA((2, SLOTS, 2)),
            ],
        ),
        compiler_params=pltpu.CompilerParams(
            dimension_semantics=("arbitrary",), vmem_limit_bytes=48 * 1024 * 1024
        ),
        cost_estimate=pl.CostEstimate(
            flops=4 * rows * (width // HEAD_SIZE) * keys * HEAD_SIZE,
            bytes_accessed=4 * rows * width + 4 * blocks * keys * HEAD_SIZE,
            transcendentals=rows * (width // HEAD_SIZE) * keys,
        ),
    )(info, row, *map(in_hbm, (queries, kv, *chosen)))


def project_kernel(depth, core, *refs):
    *a_refs, mine_ref, other_ref, o_ref, first, second = refs
    parts, rows, _ = a_refs[0].shape

    @pl.when(pl.program_id(0) == 0)
    def _():
        for to, half in ((first, core[0]), (second, 1 - core[0])):
            lanes = pl.ds(pl.multiple_of(half * depth, depth), depth)
            for chunk, a_ref in enumerate(a_refs):
                for part in range(parts):
                    at = pl.ds(chunk * rows, rows), pl.ds(part * depth, depth)
                    to[at] = a_ref[part, :, lanes]

    columns = o_ref.shape[2]
    for number in range(o_ref.shape[0]):
        at = pl.ds(number * columns, columns)
        total = sum(
            jnp.dot(
                a[...], w[:, :, at].reshape(parts * depth, columns), preferred_element_type=jnp.float32
            )
            for a, w in ((first, mine_ref), (second, other_ref))
        )
        o_ref[number] = total.astype(jnp.bfloat16)


def project(attended, mine, other, core):
    parts, part_rows, features = attended[0].shape
    rows = part_rows * len(attended)
    depth = mine.shape[1]
    columns = mine.shape[2] // parts
    together = 2
    return pl.pallas_call(
        functools.partial(project_kernel, depth),
        out_shape=jax.ShapeDtypeStruct((parts, rows, columns), jnp.bfloat16),
        grid_spec=pltpu.PrefetchScalarGridSpec(
            num_scalar_prefetch=1,
            grid=(parts // together,),
            in_specs=[
                *[pl.BlockSpec((parts, part_rows, features), lambda i, t: (0, 0, 0))] * len(attended),
                pl.BlockSpec((parts, depth, together * columns), lambda i, t: (0, 0, i)),
                pl.BlockSpec((parts, depth, together * columns), lambda i, t: (0, 0, i)),
            ],
            out_specs=pl.BlockSpec((together, rows, columns), lambda i, t: (i, 0, 0)),
            scratch_shapes=[pltpu.VMEM((rows, parts * depth), jnp.bfloat16)] * 2,
        ),
        compiler_params=pltpu.CompilerParams(
            dimension_semantics=("arbitrary",), vmem_limit_bytes=32 * 1024 * 1024
        ),
        cost_estimate=pl.CostEstimate(
            flops=2 * parts * parts * rows * features * columns,
            bytes_accessed=2 * parts * parts * features * columns + 4 * parts * rows * features,
            transcendentals=0,
        ),
    )(core, *attended, in_hbm(mine), in_hbm(other))


def gather_weight(out_weight, core):
    half = out_weight.shape[0] // 2
    mine = lax.dynamic_slice_in_dim(out_weight, core * half, half, 0)
    groups = [
        [((side ^ x_hi) * (CORES // 2) + rest) * 8 + x_hi * 4 + y for x_hi in range(2) for y in range(4)]
        for side in range(2)
        for rest in range(CORES // 2)
    ]
    return lax.all_gather(mine, ("ctx", "head"), axis=0, axis_index_groups=groups)


def per_device(queries, key_state_matrix, value_state_matrix, selected, out_weight):
    head_count = lax.axis_size("head")
    index = lax.axis_index("ctx")
    core = index % 2
    rows, width = queries.shape
    kv = jnp.concatenate([key_state_matrix, value_state_matrix], axis=1)
    other_selected = lax.ppermute(selected, "ctx", SWAP)
    mine = gather_weight(out_weight, core)
    chosen, row, place = exchange(kv, selected, other_selected, index)
    mine, chosen[-1] = lax.optimization_barrier((mine, chosen[-1]))
    other = lax.ppermute(mine, "ctx", SWAP)
    tokens = []
    share = rows // CHUNKS // head_count
    for chunk in range(CHUNKS):
        blocks = BLOCKS // CHUNKS
        attended = attention(
            queries, kv, chosen, selected.reshape(-1), row, place, chunk * blocks, blocks
        )
        tokens.append(
            lax.all_to_all(attended.reshape(head_count, share, width), "head", 0, 0, tiled=True)
        )
    mixed = lax.all_to_all(project(tokens, mine, other, core[None]), "head", 0, 0, tiled=True)
    return mixed.reshape(head_count, CHUNKS, share, -1).swapaxes(0, 1).reshape(rows, -1)


def solution(mesh):
    return jax.shard_map(
        per_device,
        mesh=mesh,
        in_specs=(
            P("ctx", "head"),
            P("ctx", "head"),
            P("ctx", "head"),
            P("ctx", None),
            P("head", None),
        ),
        out_specs=P("ctx", "head"),
        check_vma=False,
    )
```

```python
import functools

import jax
import jax.numpy as jnp
import numpy as np
from jax import lax
from jax.experimental import pallas as pl
from jax.experimental.pallas import tpu as pltpu
from jax.sharding import PartitionSpec as P

HEAD_SIZE = 128
BLOCK_TOKENS = 512
TILE = 256
SLOTS = 4
BLOCKS = 4
ROWS = BLOCKS * BLOCK_TOKENS
RING = 8
CORES = 4 * RING
EXP2_SCALE = HEAD_SIZE ** (-0.5) * 1.4426950408889634

SCHEDULE = (
    (
        (
            0, 1, 2, 3, 4, 5, 6, -1, 8, -1, 10, -1, 12, -1, -1, 15,
            16, 17, 18, 19, 20, 21, 22, -1, 24, -1, 26, -1, -1, -1, -1, -1,
        ),
        (
            -1, 1, -1, 3, -1, -1, -1, 7, -1, 9, -1, 11, -1, 13, 14, -1,
            -1, -1, -1, -1, -1, -1, -1, -1, -1, -1, -1, -1, -1, -1, -1, -1,
        ),
    ),
    (
        (
            1, 0, 3, 2, 5, -1, 7, -1, 9, -1, 11, -1, 13, -1, -1, 14,
            17, 16, 19, 18, 21, -1, 23, -1, 25, -1, 27, -1, -1, -1, -1, -1,
        ),
        (
            -1, 0, -1, -1, -1, 4, -1, 6, -1, 8, -1, 10, -1, 12, 15, -1,
            -1, -1, -1, -1, -1, -1, -1, -1, -1, -1, -1, -1, -1, -1, -1, -1,
        ),
    ),
    (
        (
            -1, 3, 0, 5, 2, -1, 4, -1, 6, -1, 8, -1, 10, -1, -1, 1,
            -1, 19, 16, 21, 18, -1, 20, 7, 22, 9, 24, 11, 1018, 13, 14, 17,
        ),
        (
            -1, 3, -1, 226, 226, -1, 36, -1, 38, -1, 40, -1, -1, 15, 12, -1,
            -1, -1, -1, -1, -1, -1, -1, -1, -1, -1, -1, -1, -1, -1, -1, -1,
        ),
    ),
    (
        (
            -1, 2, 1, -1, 3, -1, 5, -1, 7, -1, 9, -1, 11, -1, -1, 0,
            -1, 18, 17, -1, 19, 4, 21, 6, 23, 8, 25, 10, 987, 12, 15, 16,
        ),
        (
            -1, 2, 96, -1, 35, -1, 37, -1, 39, -1, 41, -1, 426, -1, 13, -1,
            -1, -1, -1, -1, -1, -1, -1, -1, -1, -1, -1, -1, -1, -1, -1, -1,
        ),
    ),
    (
        (
            -1, 5, -1, -1, 0, -1, 2, -1, 4, -1, 6, -1, 8, 1, -1, 3,
            14, 736, -1, -1, 16, 7, 18, 9, 20, 11, 22, 13, 56, 15, 12, 19,
        ),
        (
            -1, 5, -1, -1, 32, -1, 34, -1, 4, -1, -1, -1, -1, 14, 10, -1,
            -1, -1, -1, -1, -1, -1, -1, -1, -1, -1, -1, -1, -1, -1, -1, -1,
        ),
    ),
    (
        (
            -1, -1, -1, -1, 33, -1, 35, -1, 37, -1, 7, -1, 9, 0, -1, 2,
            15, 129, -1, 4, 17, 6, 51, 8, 21, 10, 23, 12, 57, 624, 13, 50,
        ),
        (
            -1, -1, -1, -1, 1, -1, 3, -1, 5, -1, 294, -1, 360, -1, 11, -1,
            -1, -1, -1, -1, -1, -1, -1, -1, -1, -1, -1, -1, -1, -1, -1, -1,
        ),
    ),
    (
        (
            -1, -1, -1, -1, -1, -1, 0, -1, 34, -1, 4, 33, 6, 3, -1, 37,
            12, 5, 14, 7, -1, 9, 48, 11, 4, 13, 20, 15, 54, 14, 10, -1,
        ),
        (
            -1, -1, -1, -1, -1, -1, 32, -1, 2, -1, -1, 1, -1, 160, 8, -1,
            -1, -1, -1, -1, -1, -1, -1, -1, -1, -1, -1, -1, -1, -1, -1, -1,
        ),
    ),
    (
        (
            -1, -1, -1, -1, -1, -1, -1, -1, -1, -1, -1, -1, 39, -1, -1, -1,
            45, 195, 15, 38, 33, 40, 611, 42, 645, 44, 53, -1, 55, 51, 43, -1,
        ),
        (
            -1, -1, -1, -1, -1, -1, -1, -1, -1, -1, -1, 32, -1, 129, 41, -1,
            -1, -1, -1, -1, -1, -1, -1, -1, -1, -1, -1, -1, -1, -1, -1, -1,
        ),
    ),
    (
        (
            -1, -1, -1, -1, -1, -1, -1, -1, -1, -1, -1, -1, 36, -1, -1, -1,
            42, 7, 44, 41, 46, 43, -1, 45, 34, 47, 36, 513, 52, -1, 40, 37,
        ),
        (
            -1, -1, -1, -1, -1, -1, -1, -1, 32, -1, -1, 35, 294, -1, 38, -1,
            -1, -1, -1, -1, -1, -1, -1, -1, -1, -1, -1, -1, -1, -1, -1, -1,
        ),
    ),
)
CHECKPOINTS = (4, 6, 7, 8)
COST = 12


def target(way, core):
    if way == 1:
        return core + CORES // 2
    side, place = divmod(core, CORES // 2)
    return side * (CORES // 2) + (place + (2 if core % 2 == 0 else -2)) % (CORES // 2)


def owners_of(item):
    if item < CORES:
        return [item] if item >= 0 else [], []
    second, first = divmod(item - CORES, CORES)
    return [], [first] + ([second - 1] if second else [])


def plan():
    found = [{core: "own", core ^ 1: "other"} for core in range(CORES)]
    parts = [{} for _ in range(CORES)]
    for step, sends in enumerate(SCHEDULE):
        for way, row in enumerate(sends):
            for core, item in enumerate(row):
                whole, wanted = owners_of(item)
                for owner in whole:
                    found[target(way, core)].setdefault(owner, (step, way))
                for position, owner in enumerate(wanted):
                    parts[target(way, core)].setdefault(owner, (step, way, position))
    return found, parts


def batches(found, parts):
    out = []
    for number, last in enumerate(CHECKPOINTS):
        first = -2 if number == 0 else CHECKPOINTS[number - 1]
        out.append(
            [
                [
                    owner
                    for owner, place in sorted((parts[core] | found[core]).items())
                    if (owner // 2 < core // 2 or owner == core ^ 1)
                    and first < (-1 if isinstance(place, str) else place[0]) <= last
                ]
                for core in range(CORES)
            ]
        )
    return out


def in_hbm(array):
    return pltpu.with_memory_space_constraint(array, pltpu.HBM)


def start_from(refs, numbers, source, first, rows, to, sem):
    for number in numbers:

        @pl.when(source == number)
        def _():
            at = pl.ds(pl.multiple_of(first, BLOCK_TOKENS), rows)
            pltpu.make_async_copy(refs[number].at[at], to, sem).start()


def wait_for(refs, source, rows, to, sem):
    @pl.when(source >= 0)
    def _():
        pltpu.make_async_copy(refs[0].at[pl.ds(0, rows)], to, sem).wait()


def move_kernel(ways, way_base, slots, slot_base, row, want, *refs):
    outs = len(ways) + (2 if slots else 0)
    ins, outs, sems = refs[: -outs - 1], refs[-outs - 1 : -1], refs[-1]

    def wanted(who, owner):
        return jnp.where(owner >= 0, want[who * CORES + jnp.maximum(owner, 0)], -1)

    jobs = []
    for way, (whole, *parts) in enumerate(ways):
        base = way_base + 5 * way
        if whole:
            jobs.append((whole, row[base], 0, ROWS, outs[way]))
        for position, numbers in enumerate(parts):
            for core in range(2 if numbers else 0):
                block = wanted(2 + 2 * way + core, row[base + 1 + 2 * position])
                to = outs[way].at[pl.ds((2 * position + core) * BLOCK_TOKENS, BLOCK_TOKENS)]
                source = jnp.where(block >= 0, row[base + 2 + 2 * position], -1)
                jobs.append((numbers, source, jnp.maximum(block, 0) * BLOCK_TOKENS, BLOCK_TOKENS, to))
    for slot, numbers in enumerate(slots):
        base = slot_base + 4 * slot
        for which in range(2):
            block = wanted(which, row[base])
            at = row[base + 2 + which]
            first = jnp.where(at >= 0, at, jnp.maximum(block, 0) * BLOCK_TOKENS)
            source = jnp.where(block >= 0, row[base + 1], -1)
            jobs.append((numbers, source, first, BLOCK_TOKENS, outs[len(ways) + which].at[slot]))
    for i, (numbers, source, first, rows, to) in enumerate(jobs):
        start_from(ins, numbers, source, first, rows, to, sems.at[i])
    for i, (numbers, source, first, rows, to) in enumerate(jobs):
        wait_for(ins, source, rows, to, sems.at[i])


def move(ways, slots, scalars, arrays, width, after=()):
    out_shapes = [(ROWS, width)] * len(ways[0]) + [(len(slots[0]), BLOCK_TOKENS, width)] * (2 if slots[0] else 0)

    def whole(shape):
        return pl.BlockSpec(shape, lambda *_: (0,) * len(shape))

    return pl.pallas_call(
        functools.partial(move_kernel, *ways, *slots),
        out_shape=[
            pltpu.HBM(s, arrays[0].dtype) if len(s) == 3 else jax.ShapeDtypeStruct(s, arrays[0].dtype)
            for s in out_shapes
        ],
        grid_spec=pltpu.PrefetchScalarGridSpec(
            num_scalar_prefetch=len(scalars),
            grid=(1,),
            in_specs=[pl.BlockSpec(memory_space=pltpu.HBM)] * (len(arrays) + len(after)),
            out_specs=[whole(s) for s in out_shapes],
            scratch_shapes=[pltpu.SemaphoreType.DMA((5 * len(ways[0]) + 2 * len(slots[0]),))],
        ),
        compiler_params=pltpu.CompilerParams(vmem_limit_bytes=24 * 1024 * 1024),
        cost_estimate=pl.CostEstimate(
            flops=0,
            bytes_accessed=4 * COST * sum(int(np.prod(s)) for s in out_shapes),
            transcendentals=0,
        ),
    )(*scalars, *arrays, *after)


class Plan:
    def __init__(self):
        found, parts = plan()
        groups = batches(found, parts)
        columns = []
        self.ways, self.slots, self.sources = {}, {}, {}

        def number_of(place, sources):
            if place not in sources:
                sources.append(place)
            return sources.index(place)

        def add(table):
            base = sum(c.shape[1] for c in columns)
            columns.append(table.reshape(CORES, -1))
            return base

        for step in range(1, len(SCHEDULE)):
            sources, numbers = self.sources.setdefault(step, []), []
            table = np.full((CORES, 2, 5), -1, np.int32)
            for way in range(2):
                used = [set(), set(), set()]
                for core, item in enumerate(SCHEDULE[step][way]):
                    whole, wanted = owners_of(item)
                    for owner in whole:
                        table[core, way, 0] = number_of(found[core][owner], sources)
                        used[0].add(int(table[core, way, 0]))
                    for i, owner in enumerate(wanted):
                        number = number_of(found[core][owner], sources)
                        table[core, way, 1 + 2 * i : 3 + 2 * i] = owner, number
                        used[1 + i].add(number)
                numbers.append(tuple(tuple(sorted(n)) for n in used))
            self.ways[step] = (tuple(numbers), add(table))

        held = np.full((CORES, CORES, 2), -1, np.int32)
        for batch, group in enumerate(groups):
            depth = max(len(owners) for owners in group)
            step = CHECKPOINTS[batch] + 2
            sources, numbers = self.sources.setdefault(step, []), [set() for _ in range(depth)]
            table = np.full((CORES, depth, 4), -1, np.int32)
            for core, owners in enumerate(group):
                for slot, owner in enumerate(owners):
                    held[core, owner] = (batch, slot)
                    if owner in found[core]:
                        number = number_of(found[core][owner], sources)
                        table[core, slot, :2] = owner, number
                    else:
                        *place, position = parts[core][owner]
                        number = number_of(tuple(place), sources)
                        rows = [(2 * position + c) * BLOCK_TOKENS for c in (core % 2, 1 - core % 2)]
                        table[core, slot] = owner, number, *rows
                    numbers[slot].add(number)
            self.slots[step] = (tuple(tuple(sorted(n)) for n in numbers), add(table))
        place = held.copy()
        for core in range(CORES):
            for owner in range(CORES):
                if held[core, owner, 0] < 0 <= held[core ^ 1, owner, 0]:
                    place[core, owner] = held[core ^ 1, owner]
                    place[core, owner, 0] += len(CHECKPOINTS)
        self.place = add(place)
        self.table = np.concatenate(columns, axis=1)


SWAP = [(i, i ^ 1) for i in range(CORES)]


def exchange(kv, selected, other_selected, index):
    tables = Plan()
    row = jnp.asarray(tables.table)[index]
    arrived = {"own": kv, "other": lax.ppermute(kv, "ctx", SWAP)}

    def pairs(step, way):
        return [(a, target(way, a)) for a, owner in enumerate(SCHEDULE[step][way]) if owner >= 0]

    mine, other = selected.reshape(1, -1), other_selected.reshape(1, -1)
    chip = jnp.where(index % 2 == 0, jnp.concatenate([mine, other]), jnp.concatenate([other, mine]))
    along, across = (
        lax.ppermute(chip, "ctx", [(target(way, i), i) for i in range(CORES >> way)]) for way in range(2)
    )
    choices = jnp.concatenate([mine, other, along, across])[:, None, :]
    owner = jnp.arange(CORES, dtype=jnp.int32)[None, :, None]
    named = (choices >= 0) & (choices // BLOCKS == owner)
    want = jnp.max(jnp.where(named, choices % BLOCKS, -1), axis=2).reshape(-1)

    kept, passed = [], []
    for step in range(CHECKPOINTS[-1] + 3):
        none = ((), 0)
        ways, slots = tables.ways.get(step, none), tables.slots.get(step, none)
        if step == 0:
            buffers = [kv, kv]
        elif ways[0] or slots[0]:
            buffers = move(
                ways,
                slots,
                [row, want if step > 1 else row],
                [arrived[key] for key in tables.sources[step]],
                kv.shape[1],
                after=buffers[:1] if step <= len(SCHEDULE) else passed,
            )
        else:
            continue
        if step < len(SCHEDULE):
            for way in range(2):
                arrived[step, way] = lax.ppermute(buffers[way], "ctx", pairs(step, way))
        if slots[0]:
            keep, give = buffers[-2:]
            kept.append(keep)
            passed.append(lax.ppermute(give, "ctx", SWAP))
    return kept + passed, row, tables.place


def attention_kernel(q_heads, sources, place, info, row_ref, q_ref, kv_ref, *refs):
    chosen, (o_ref, keys, values, sems) = refs[:sources], refs[sources:]
    step = pl.program_id(0)
    steps = pl.num_programs(0)
    here = lax.rem(step, 2)
    own_to = pl.ds((SLOTS - 1) * BLOCK_TOKENS, BLOCK_TOKENS)

    def pair(block_ref, to, buf, slot):
        return (
            pltpu.make_async_copy(
                block_ref.at[:, pl.ds(0, HEAD_SIZE)], keys.at[buf, to], sems.at[buf, slot, 0]
            ),
            pltpu.make_async_copy(
                block_ref.at[:, pl.ds(HEAD_SIZE, HEAD_SIZE)],
                values.at[buf, to, pl.ds(0, HEAD_SIZE)],
                sems.at[buf, slot, 1],
            ),
        )

    def own_rows(at):
        return kv_ref.at[pl.ds(pl.multiple_of(at * BLOCK_TOKENS, BLOCK_TOKENS), BLOCK_TOKENS)]

    def choice(at, slot):
        block = info[at * (SLOTS - 1) + slot]
        owner = jnp.maximum(block, 0) // BLOCKS
        return jnp.where(block < 0, -1, row_ref[place + 2 * owner]), row_ref[place + 2 * owner + 1]

    def start(at, buf):
        for copy in pair(own_rows(at), own_to, buf, SLOTS - 1):
            copy.start()
        for slot in range(SLOTS - 1):
            to = pl.ds(slot * BLOCK_TOKENS, BLOCK_TOKENS)
            array, block = choice(at, slot)
            for number in range(sources):

                @pl.when(array == number)
                def _():
                    for copy in pair(chosen[number].at[block], to, buf, slot):
                        copy.start()

    @pl.when(step == 0)
    def _():
        start(step, here)

    @pl.when(step + 1 < steps)
    def _():
        start(step + 1, 1 - here)

    values[here, :, pl.ds(HEAD_SIZE, HEAD_SIZE)] = jnp.ones(
        (SLOTS * BLOCK_TOKENS, HEAD_SIZE), jnp.bfloat16
    )
    for copy in pair(own_rows(step), own_to, here, SLOTS - 1):
        copy.wait()
    for slot in range(SLOTS - 1):
        to = pl.ds(slot * BLOCK_TOKENS, BLOCK_TOKENS)
        array, _ = choice(step, slot)

        @pl.when(array >= 0)
        def _():
            for copy in pair(own_rows(step), to, here, slot):
                copy.wait()

        @pl.when(array < 0)
        def _():
            first = keys[here, pl.ds((SLOTS - 1) * BLOCK_TOKENS, 16), :][0:1, :]
            keys[here, to, :] = jnp.broadcast_to(first, (BLOCK_TOKENS, HEAD_SIZE))
            values[here, to, :] = jnp.zeros((BLOCK_TOKENS, 2 * HEAD_SIZE), jnp.bfloat16)

    row = lax.broadcasted_iota(jnp.int32, (TILE, TILE), 0)
    col = lax.broadcasted_iota(jnp.int32, (TILE, TILE), 1)
    causal = row >= col
    dims = (((1,), (1,)), ((), ()))

    units = [(head, tile) for head in range(q_heads) for tile in range(BLOCK_TOKENS // TILE)]

    def places(unit):
        head, tile = unit
        far = (SLOTS - 1) * BLOCK_TOKENS + tile * TILE
        return pl.ds(tile * TILE, TILE), pl.ds(head * HEAD_SIZE, HEAD_SIZE), pl.ds(0, far), pl.ds(far, TILE)

    def scores(unit):
        rows, lanes, *parts = places(unit)
        query = q_ref[rows, lanes]
        far, near = (
            lax.dot_general(query, keys[here, at, :], dims, preferred_element_type=jnp.float32)
            for at in parts
        )
        return far, jnp.where(causal, near, -1e30)

    following = scores(units[0])
    for number, unit in enumerate(units):
        now = following
        if number + 1 < len(units):
            following = scores(units[number + 1])
        rows, lanes, *parts = places(unit)
        highest = functools.reduce(jnp.maximum, [jnp.max(s, axis=1, keepdims=True) for s in now])
        total = sum(
            jnp.dot(
                jnp.exp2((s - highest) * EXP2_SCALE).astype(jnp.bfloat16),
                values[here, at, :],
                preferred_element_type=jnp.float32,
            )
            for s, at in zip(now, parts)
        )
        o_ref[rows, lanes] = (total[:, :HEAD_SIZE] / total[:, HEAD_SIZE:]).astype(jnp.bfloat16)


def attention(queries, kv, chosen, info, row, place):
    rows, width = queries.shape
    blocks = rows // BLOCK_TOKENS
    keys = SLOTS * BLOCK_TOKENS
    return pl.pallas_call(
        functools.partial(attention_kernel, width // HEAD_SIZE, len(chosen), place),
        out_shape=jax.ShapeDtypeStruct((rows, width), jnp.bfloat16),
        grid_spec=pltpu.PrefetchScalarGridSpec(
            num_scalar_prefetch=2,
            grid=(blocks,),
            in_specs=[pl.BlockSpec((BLOCK_TOKENS, width), lambda i, *_: (i, 0))]
            + [pl.BlockSpec(memory_space=pltpu.HBM)] * (1 + len(chosen)),
            out_specs=pl.BlockSpec((BLOCK_TOKENS, width), lambda i, *_: (i, 0)),
            scratch_shapes=[
                pltpu.VMEM((2, keys, HEAD_SIZE), jnp.bfloat16),
                pltpu.VMEM((2, keys, 2 * HEAD_SIZE), jnp.bfloat16),
                pltpu.SemaphoreType.DMA((2, SLOTS, 2)),
            ],
        ),
        compiler_params=pltpu.CompilerParams(
            dimension_semantics=("arbitrary",), vmem_limit_bytes=48 * 1024 * 1024
        ),
        cost_estimate=pl.CostEstimate(
            flops=4 * rows * (width // HEAD_SIZE) * keys * HEAD_SIZE,
            bytes_accessed=4 * rows * width + 4 * blocks * keys * HEAD_SIZE,
            transcendentals=rows * (width // HEAD_SIZE) * keys,
        ),
    )(info, row, *map(in_hbm, (queries, kv, *chosen)))


def project_kernel(depth, core, a_ref, mine_ref, other_ref, o_ref, first, second):
    parts, rows, _ = a_ref.shape

    @pl.when(pl.program_id(0) == 0)
    def _():
        for to, half in ((first, core[0]), (second, 1 - core[0])):
            lanes = pl.ds(pl.multiple_of(half * depth, depth), depth)
            for part in range(parts):
                to[:, pl.ds(part * depth, depth)] = a_ref[part, :, lanes]

    columns = o_ref.shape[2]
    for number in range(o_ref.shape[0]):
        at = pl.ds(number * columns, columns)
        total = sum(
            jnp.dot(
                a[...], w[:, :, at].reshape(parts * depth, columns), preferred_element_type=jnp.float32
            )
            for a, w in ((first, mine_ref), (second, other_ref))
        )
        o_ref[number] = total.astype(jnp.bfloat16)


def project(attended, mine, other, core):
    parts, rows, features = attended.shape
    depth = mine.shape[1]
    columns = mine.shape[2] // parts
    together = 2
    return pl.pallas_call(
        functools.partial(project_kernel, depth),
        out_shape=jax.ShapeDtypeStruct((parts, rows, columns), jnp.bfloat16),
        grid_spec=pltpu.PrefetchScalarGridSpec(
            num_scalar_prefetch=1,
            grid=(parts // together,),
            in_specs=[
                pl.BlockSpec((parts, rows, features), lambda i, t: (0, 0, 0)),
                pl.BlockSpec((parts, depth, together * columns), lambda i, t: (0, 0, i)),
                pl.BlockSpec((parts, depth, together * columns), lambda i, t: (0, 0, i)),
            ],
            out_specs=pl.BlockSpec((together, rows, columns), lambda i, t: (i, 0, 0)),
            scratch_shapes=[pltpu.VMEM((rows, parts * depth), jnp.bfloat16)] * 2,
        ),
        compiler_params=pltpu.CompilerParams(
            dimension_semantics=("arbitrary",), vmem_limit_bytes=32 * 1024 * 1024
        ),
        cost_estimate=pl.CostEstimate(
            flops=2 * parts * parts * rows * features * columns,
            bytes_accessed=2 * parts * parts * features * columns + 4 * parts * rows * features,
            transcendentals=0,
        ),
    )(core, attended, in_hbm(mine), in_hbm(other))


def gather_weight(out_weight, core):
    half = out_weight.shape[0] // 2
    mine = lax.dynamic_slice_in_dim(out_weight, core * half, half, 0)
    groups = [
        [((side ^ x_hi) * (CORES // 2) + rest) * 8 + x_hi * 4 + y for x_hi in range(2) for y in range(4)]
        for side in range(2)
        for rest in range(CORES // 2)
    ]
    return lax.all_gather(mine, ("ctx", "head"), axis=0, axis_index_groups=groups)


def per_device(queries, key_state_matrix, value_state_matrix, selected, out_weight):
    head_count = lax.axis_size("head")
    index = lax.axis_index("ctx")
    core = index % 2
    rows, width = queries.shape
    kv = jnp.concatenate([key_state_matrix, value_state_matrix], axis=1)
    other_selected = lax.ppermute(selected, "ctx", SWAP)
    mine = gather_weight(out_weight, core)
    chosen, row, place = exchange(kv, selected, other_selected, index)
    mine, chosen[-1] = lax.optimization_barrier((mine, chosen[-1]))
    other = lax.ppermute(mine, "ctx", SWAP)
    attended = attention(queries, kv, chosen, selected.reshape(-1), row, place)
    tokens = lax.all_to_all(
        attended.reshape(head_count, rows // head_count, width), "head", 0, 0, tiled=True
    )
    mixed = project(tokens, mine, other, core[None])
    return lax.all_to_all(mixed, "head", 0, 0, tiled=True).reshape(rows, -1)


def solution(mesh):
    return jax.shard_map(
        per_device,
        mesh=mesh,
        in_specs=(
            P("ctx", "head"),
            P("ctx", "head"),
            P("ctx", "head"),
            P("ctx", None),
            P("head", None),
        ),
        out_specs=P("ctx", "head"),
        check_vma=False,
    )
```

```python
import functools

import jax
import jax.numpy as jnp
import numpy as np
from jax import lax
from jax.experimental import pallas as pl
from jax.experimental.pallas import tpu as pltpu
from jax.sharding import PartitionSpec as P

HEAD_SIZE = 128
BLOCK_TOKENS = 512
TILE = 256
SLOTS = 4
BLOCKS = 4
ROWS = BLOCKS * BLOCK_TOKENS
RING = 8
CORES = 4 * RING
EXP2_SCALE = HEAD_SIZE ** (-0.5) * 1.4426950408889634

SCHEDULE = (
    (
        (
            0, 1, 2, 3, 4, 5, 6, -1, 8, -1, 10, -1, 12, -1, -1, 15,
            16, 17, 18, 19, 20, 21, 22, -1, 24, -1, 26, -1, -1, -1, -1, -1,
        ),
        (
            -1, 1, -1, 3, -1, -1, -1, 7, -1, 9, -1, 11, -1, 13, 14, -1,
            -1, -1, -1, -1, -1, -1, -1, -1, -1, -1, -1, -1, -1, -1, -1, -1,
        ),
    ),
    (
        (
            1, 0, 3, 2, 5, -1, 7, -1, 9, -1, 11, -1, 13, -1, -1, 14,
            17, 16, 19, 18, 21, -1, 23, -1, 25, -1, 27, -1, -1, -1, -1, -1,
        ),
        (
            -1, 0, -1, -1, -1, 4, -1, 6, -1, 8, -1, 10, -1, 12, 15, -1,
            -1, -1, -1, -1, -1, -1, -1, -1, -1, -1, -1, -1, -1, -1, -1, -1,
        ),
    ),
    (
        (
            -1, 3, 0, 5, 2, -1, 4, -1, 6, -1, 8, -1, 10, -1, -1, 1,
            -1, 19, 16, 21, 18, -1, 20, 7, 22, 9, 24, 11, 1018, 13, 14, 17,
        ),
        (
            -1, 3, -1, 226, 226, -1, 36, -1, 38, -1, 40, -1, -1, 15, 12, -1,
            -1, -1, -1, -1, -1, -1, -1, -1, -1, -1, -1, -1, -1, -1, -1, -1,
        ),
    ),
    (
        (
            -1, 2, 1, -1, 3, -1, 5, -1, 7, -1, 9, -1, 11, -1, -1, 0,
            -1, 18, 17, -1, 19, 4, 21, 6, 23, 8, 25, 10, 987, 12, 15, 16,
        ),
        (
            -1, 2, 96, -1, 35, -1, 37, -1, 39, -1, 41, -1, 426, -1, 13, -1,
            -1, -1, -1, -1, -1, -1, -1, -1, -1, -1, -1, -1, -1, -1, -1, -1,
        ),
    ),
    (
        (
            -1, 5, -1, -1, 0, -1, 2, -1, 4, -1, 6, -1, 8, 1, -1, 3,
            14, 736, -1, -1, 16, 7, 18, 9, 20, 11, 22, 13, 56, 15, 12, 19,
        ),
        (
            -1, 5, -1, -1, 32, -1, 34, -1, 4, -1, -1, -1, -1, 14, 10, -1,
            -1, -1, -1, -1, -1, -1, -1, -1, -1, -1, -1, -1, -1, -1, -1, -1,
        ),
    ),
    (
        (
            -1, -1, -1, -1, 33, -1, 35, -1, 37, -1, 7, -1, 9, 0, -1, 2,
            15, 129, -1, 4, 17, 6, 51, 8, 21, 10, 23, 12, 57, 624, 13, 50,
        ),
        (
            -1, -1, -1, -1, 1, -1, 3, -1, 5, -1, 294, -1, 360, -1, 11, -1,
            -1, -1, -1, -1, -1, -1, -1, -1, -1, -1, -1, -1, -1, -1, -1, -1,
        ),
    ),
    (
        (
            -1, -1, -1, -1, -1, -1, 0, -1, 34, -1, 4, 33, 6, 3, -1, 37,
            12, 5, 14, 7, -1, 9, 48, 11, 4, 13, 20, 15, 54, 14, 10, -1,
        ),
        (
            -1, -1, -1, -1, -1, -1, 32, -1, 2, -1, -1, 1, -1, 160, 8, -1,
            -1, -1, -1, -1, -1, -1, -1, -1, -1, -1, -1, -1, -1, -1, -1, -1,
        ),
    ),
    (
        (
            -1, -1, -1, -1, -1, -1, -1, -1, -1, -1, -1, -1, 39, -1, -1, -1,
            45, 195, 15, 38, 33, 40, 611, 42, 645, 44, 53, -1, 55, 51, 43, -1,
        ),
        (
            -1, -1, -1, -1, -1, -1, -1, -1, -1, -1, -1, 32, -1, 129, 41, -1,
            -1, -1, -1, -1, -1, -1, -1, -1, -1, -1, -1, -1, -1, -1, -1, -1,
        ),
    ),
    (
        (
            -1, -1, -1, -1, -1, -1, -1, -1, -1, -1, -1, -1, 36, -1, -1, -1,
            42, 7, 44, 41, 46, 43, -1, 45, 34, 47, 36, 513, 52, -1, 40, 37,
        ),
        (
            -1, -1, -1, -1, -1, -1, -1, -1, 32, -1, -1, 35, 294, -1, 38, -1,
            -1, -1, -1, -1, -1, -1, -1, -1, -1, -1, -1, -1, -1, -1, -1, -1,
        ),
    ),
)
CHECKPOINTS = (3, 5, 7, 8)
COST = 12


def target(way, core):
    if way == 1:
        return core + CORES // 2
    side, place = divmod(core, CORES // 2)
    return side * (CORES // 2) + (place + (2 if core % 2 == 0 else -2)) % (CORES // 2)


def owners_of(item):
    if item < CORES:
        return [item] if item >= 0 else [], []
    second, first = divmod(item - CORES, CORES)
    return [], [first] + ([second - 1] if second else [])


def plan():
    found = [{core: "own", core ^ 1: "other"} for core in range(CORES)]
    parts = [{} for _ in range(CORES)]
    for step, sends in enumerate(SCHEDULE):
        for way, row in enumerate(sends):
            for core, item in enumerate(row):
                whole, wanted = owners_of(item)
                for owner in whole:
                    found[target(way, core)].setdefault(owner, (step, way))
                for position, owner in enumerate(wanted):
                    parts[target(way, core)].setdefault(owner, (step, way, position))
    return found, parts


def batches(found, parts):
    out = []
    for number, last in enumerate(CHECKPOINTS):
        first = -2 if number == 0 else CHECKPOINTS[number - 1]
        out.append(
            [
                [
                    owner
                    for owner, place in sorted((parts[core] | found[core]).items())
                    if (owner // 2 < core // 2 or owner == core ^ 1)
                    and first < (-1 if isinstance(place, str) else place[0]) <= last
                ]
                for core in range(CORES)
            ]
        )
    return out


def in_hbm(array):
    return pltpu.with_memory_space_constraint(array, pltpu.HBM)


def start_from(refs, numbers, source, first, rows, to, sem):
    for number in numbers:

        @pl.when(source == number)
        def _():
            at = pl.ds(pl.multiple_of(first, BLOCK_TOKENS), rows)
            pltpu.make_async_copy(refs[number].at[at], to, sem).start()


def wait_for(refs, source, rows, to, sem):
    @pl.when(source >= 0)
    def _():
        pltpu.make_async_copy(refs[0].at[pl.ds(0, rows)], to, sem).wait()


def move_kernel(ways, way_base, slots, slot_base, row, want, *refs):
    outs = len(ways) + (2 if slots else 0)
    ins, outs, sems = refs[: -outs - 1], refs[-outs - 1 : -1], refs[-1]

    def wanted(who, owner):
        return jnp.where(owner >= 0, want[who * CORES + jnp.maximum(owner, 0)], -1)

    jobs = []
    for way, (whole, *parts) in enumerate(ways):
        base = way_base + 5 * way
        if whole:
            jobs.append((whole, row[base], 0, ROWS, outs[way]))
        for position, numbers in enumerate(parts):
            for core in range(2 if numbers else 0):
                block = wanted(2 + 2 * way + core, row[base + 1 + 2 * position])
                to = outs[way].at[pl.ds((2 * position + core) * BLOCK_TOKENS, BLOCK_TOKENS)]
                source = jnp.where(block >= 0, row[base + 2 + 2 * position], -1)
                jobs.append((numbers, source, jnp.maximum(block, 0) * BLOCK_TOKENS, BLOCK_TOKENS, to))
    for slot, numbers in enumerate(slots):
        base = slot_base + 4 * slot
        for which in range(2):
            block = wanted(which, row[base])
            at = row[base + 2 + which]
            first = jnp.where(at >= 0, at, jnp.maximum(block, 0) * BLOCK_TOKENS)
            source = jnp.where(block >= 0, row[base + 1], -1)
            jobs.append((numbers, source, first, BLOCK_TOKENS, outs[len(ways) + which].at[slot]))
    for i, (numbers, source, first, rows, to) in enumerate(jobs):
        start_from(ins, numbers, source, first, rows, to, sems.at[i])
    for i, (numbers, source, first, rows, to) in enumerate(jobs):
        wait_for(ins, source, rows, to, sems.at[i])


def move(ways, slots, scalars, arrays, width, after=()):
    out_shapes = [(ROWS, width)] * len(ways[0]) + [(len(slots[0]), BLOCK_TOKENS, width)] * (2 if slots[0] else 0)

    kept = len(ways[0])

    def whole(shape):
        return pl.BlockSpec(shape, lambda *_: (0,) * len(shape))

    return pl.pallas_call(
        functools.partial(move_kernel, *ways, *slots),
        out_shape=[
            pltpu.HBM(s, arrays[0].dtype) if i == kept else jax.ShapeDtypeStruct(s, arrays[0].dtype)
            for i, s in enumerate(out_shapes)
        ],
        grid_spec=pltpu.PrefetchScalarGridSpec(
            num_scalar_prefetch=len(scalars),
            grid=(1,),
            in_specs=[pl.BlockSpec(memory_space=pltpu.HBM)] * (len(arrays) + len(after)),
            out_specs=[whole(s) for s in out_shapes],
            scratch_shapes=[pltpu.SemaphoreType.DMA((5 * len(ways[0]) + 2 * len(slots[0]),))],
        ),
        compiler_params=pltpu.CompilerParams(vmem_limit_bytes=24 * 1024 * 1024),
        cost_estimate=pl.CostEstimate(
            flops=0,
            bytes_accessed=4 * COST * sum(int(np.prod(s)) for s in out_shapes),
            transcendentals=0,
        ),
    )(*scalars, *arrays, *after)


class Plan:
    def __init__(self):
        found, parts = plan()
        groups = batches(found, parts)
        columns = []
        self.ways, self.slots, self.sources = {}, {}, {}

        def number_of(place, sources):
            if place not in sources:
                sources.append(place)
            return sources.index(place)

        def add(table):
            base = sum(c.shape[1] for c in columns)
            columns.append(table.reshape(CORES, -1))
            return base

        for step in range(1, len(SCHEDULE)):
            sources, numbers = self.sources.setdefault(step, []), []
            table = np.full((CORES, 2, 5), -1, np.int32)
            for way in range(2):
                used = [set(), set(), set()]
                for core, item in enumerate(SCHEDULE[step][way]):
                    whole, wanted = owners_of(item)
                    for owner in whole:
                        table[core, way, 0] = number_of(found[core][owner], sources)
                        used[0].add(int(table[core, way, 0]))
                    for i, owner in enumerate(wanted):
                        number = number_of(found[core][owner], sources)
                        table[core, way, 1 + 2 * i : 3 + 2 * i] = owner, number
                        used[1 + i].add(number)
                numbers.append(tuple(tuple(sorted(n)) for n in used))
            self.ways[step] = (tuple(numbers), add(table))

        held = np.full((CORES, CORES, 2), -1, np.int32)
        for batch, group in enumerate(groups):
            depth = max(len(owners) for owners in group)
            step = CHECKPOINTS[batch] + 2
            sources, numbers = self.sources.setdefault(step, []), [set() for _ in range(depth)]
            table = np.full((CORES, depth, 4), -1, np.int32)
            for core, owners in enumerate(group):
                for slot, owner in enumerate(owners):
                    held[core, owner] = (batch, slot)
                    if owner in found[core]:
                        number = number_of(found[core][owner], sources)
                        table[core, slot, :2] = owner, number
                    else:
                        *place, position = parts[core][owner]
                        number = number_of(tuple(place), sources)
                        rows = [(2 * position + c) * BLOCK_TOKENS for c in (core % 2, 1 - core % 2)]
                        table[core, slot] = owner, number, *rows
                    numbers[slot].add(number)
            self.slots[step] = (tuple(tuple(sorted(n)) for n in numbers), add(table))
        place = held.copy()
        for core in range(CORES):
            for owner in range(CORES):
                if held[core, owner, 0] < 0 <= held[core ^ 1, owner, 0]:
                    place[core, owner] = held[core ^ 1, owner]
                    place[core, owner, 0] += len(CHECKPOINTS)
        self.place = add(place)
        self.table = np.concatenate(columns, axis=1)


SWAP = [(i, i ^ 1) for i in range(CORES)]


def exchange(kv, selected, other_selected, index):
    tables = Plan()
    row = jnp.asarray(tables.table)[index]
    arrived = {"own": kv, "other": lax.ppermute(kv, "ctx", SWAP)}

    def pairs(step, way):
        return [(a, target(way, a)) for a, owner in enumerate(SCHEDULE[step][way]) if owner >= 0]

    mine, other = selected.reshape(1, -1), other_selected.reshape(1, -1)
    chip = jnp.where(index % 2 == 0, jnp.concatenate([mine, other]), jnp.concatenate([other, mine]))
    along, across = (
        lax.ppermute(chip, "ctx", [(target(way, i), i) for i in range(CORES >> way)]) for way in range(2)
    )
    choices = jnp.concatenate([mine, other, along, across])[:, None, :]
    owner = jnp.arange(CORES, dtype=jnp.int32)[None, :, None]
    named = (choices >= 0) & (choices // BLOCKS == owner)
    want = jnp.max(jnp.where(named, choices % BLOCKS, -1), axis=2).reshape(-1)

    kept, passed = [], []
    for step in range(CHECKPOINTS[-1] + 3):
        none = ((), 0)
        ways, slots = tables.ways.get(step, none), tables.slots.get(step, none)
        if step == 0:
            buffers = [kv, kv]
        elif ways[0] or slots[0]:
            buffers = move(
                ways,
                slots,
                [row, want if step > 1 else row],
                [arrived[key] for key in tables.sources[step]],
                kv.shape[1],
                after=buffers[:1] if step <= len(SCHEDULE) else passed,
            )
        else:
            continue
        if step < len(SCHEDULE):
            for way in range(2):
                arrived[step, way] = lax.ppermute(buffers[way], "ctx", pairs(step, way))
        if slots[0]:
            keep, give = buffers[-2:]
            kept.append(keep)
            passed.append(lax.ppermute(give, "ctx", SWAP))
    return kept + passed, row, tables.place


def attention_kernel(q_heads, sources, place, info, row_ref, q_ref, kv_ref, *refs):
    chosen, (o_ref, keys, values, sems) = refs[:sources], refs[sources:]
    step = pl.program_id(0)
    steps = pl.num_programs(0)
    here = lax.rem(step, 2)
    own_to = pl.ds((SLOTS - 1) * BLOCK_TOKENS, BLOCK_TOKENS)

    def pair(block_ref, to, buf, slot):
        return (
            pltpu.make_async_copy(
                block_ref.at[:, pl.ds(0, HEAD_SIZE)], keys.at[buf, to], sems.at[buf, slot, 0]
            ),
            pltpu.make_async_copy(
                block_ref.at[:, pl.ds(HEAD_SIZE, HEAD_SIZE)],
                values.at[buf, to, pl.ds(0, HEAD_SIZE)],
                sems.at[buf, slot, 1],
            ),
        )

    def own_rows(at):
        return kv_ref.at[pl.ds(pl.multiple_of(at * BLOCK_TOKENS, BLOCK_TOKENS), BLOCK_TOKENS)]

    def choice(at, slot):
        block = info[at * (SLOTS - 1) + slot]
        owner = jnp.maximum(block, 0) // BLOCKS
        return jnp.where(block < 0, -1, row_ref[place + 2 * owner]), row_ref[place + 2 * owner + 1]

    def start(at, buf):
        for copy in pair(own_rows(at), own_to, buf, SLOTS - 1):
            copy.start()
        for slot in range(SLOTS - 1):
            to = pl.ds(slot * BLOCK_TOKENS, BLOCK_TOKENS)
            array, block = choice(at, slot)
            for number in range(sources):

                @pl.when(array == number)
                def _():
                    for copy in pair(chosen[number].at[block], to, buf, slot):
                        copy.start()

    @pl.when(step == 0)
    def _():
        start(step, here)

    @pl.when(step + 1 < steps)
    def _():
        start(step + 1, 1 - here)

    values[here, :, pl.ds(HEAD_SIZE, HEAD_SIZE)] = jnp.ones(
        (SLOTS * BLOCK_TOKENS, HEAD_SIZE), jnp.bfloat16
    )
    for copy in pair(own_rows(step), own_to, here, SLOTS - 1):
        copy.wait()
    for slot in range(SLOTS - 1):
        to = pl.ds(slot * BLOCK_TOKENS, BLOCK_TOKENS)
        array, _ = choice(step, slot)

        @pl.when(array >= 0)
        def _():
            for copy in pair(own_rows(step), to, here, slot):
                copy.wait()

        @pl.when(array < 0)
        def _():
            first = keys[here, pl.ds((SLOTS - 1) * BLOCK_TOKENS, 16), :][0:1, :]
            keys[here, to, :] = jnp.broadcast_to(first, (BLOCK_TOKENS, HEAD_SIZE))
            values[here, to, :] = jnp.zeros((BLOCK_TOKENS, 2 * HEAD_SIZE), jnp.bfloat16)

    row = lax.broadcasted_iota(jnp.int32, (TILE, TILE), 0)
    col = lax.broadcasted_iota(jnp.int32, (TILE, TILE), 1)
    causal = row >= col
    dims = (((1,), (1,)), ((), ()))

    units = [(head, tile) for head in range(q_heads) for tile in range(BLOCK_TOKENS // TILE)]

    def places(unit):
        head, tile = unit
        far = (SLOTS - 1) * BLOCK_TOKENS + tile * TILE
        return pl.ds(tile * TILE, TILE), pl.ds(head * HEAD_SIZE, HEAD_SIZE), pl.ds(0, far), pl.ds(far, TILE)

    def scores(unit):
        rows, lanes, *parts = places(unit)
        query = q_ref[rows, lanes]
        far, near = (
            lax.dot_general(query, keys[here, at, :], dims, preferred_element_type=jnp.float32)
            for at in parts
        )
        return far, jnp.where(causal, near, -1e30)

    following = scores(units[0])
    for number, unit in enumerate(units):
        now = following
        if number + 1 < len(units):
            following = scores(units[number + 1])
        rows, lanes, *parts = places(unit)
        highest = functools.reduce(jnp.maximum, [jnp.max(s, axis=1, keepdims=True) for s in now])
        total = sum(
            jnp.dot(
                jnp.exp2((s - highest) * EXP2_SCALE).astype(jnp.bfloat16),
                values[here, at, :],
                preferred_element_type=jnp.float32,
            )
            for s, at in zip(now, parts)
        )
        o_ref[rows, lanes] = (total[:, :HEAD_SIZE] / total[:, HEAD_SIZE:]).astype(jnp.bfloat16)


def attention(queries, kv, chosen, info, row, place):
    rows, width = queries.shape
    blocks = rows // BLOCK_TOKENS
    keys = SLOTS * BLOCK_TOKENS
    return pl.pallas_call(
        functools.partial(attention_kernel, width // HEAD_SIZE, len(chosen), place),
        out_shape=jax.ShapeDtypeStruct((rows, width), jnp.bfloat16),
        grid_spec=pltpu.PrefetchScalarGridSpec(
            num_scalar_prefetch=2,
            grid=(blocks,),
            in_specs=[pl.BlockSpec((BLOCK_TOKENS, width), lambda i, *_: (i, 0))]
            + [pl.BlockSpec(memory_space=pltpu.HBM)] * (1 + len(chosen)),
            out_specs=pl.BlockSpec((BLOCK_TOKENS, width), lambda i, *_: (i, 0)),
            scratch_shapes=[
                pltpu.VMEM((2, keys, HEAD_SIZE), jnp.bfloat16),
                pltpu.VMEM((2, keys, 2 * HEAD_SIZE), jnp.bfloat16),
                pltpu.SemaphoreType.DMA((2, SLOTS, 2)),
            ],
        ),
        compiler_params=pltpu.CompilerParams(
            dimension_semantics=("arbitrary",), vmem_limit_bytes=48 * 1024 * 1024
        ),
        cost_estimate=pl.CostEstimate(
            flops=4 * rows * (width // HEAD_SIZE) * keys * HEAD_SIZE,
            bytes_accessed=4 * rows * width + 4 * blocks * keys * HEAD_SIZE,
            transcendentals=rows * (width // HEAD_SIZE) * keys,
        ),
    )(info, row, *map(in_hbm, (queries, kv, *chosen)))


def project_kernel(depth, core, a_ref, mine_ref, other_ref, o_ref, first, second):
    parts, rows, _ = a_ref.shape

    @pl.when(pl.program_id(0) == 0)
    def _():
        for to, half in ((first, core[0]), (second, 1 - core[0])):
            lanes = pl.ds(pl.multiple_of(half * depth, depth), depth)
            for part in range(parts):
                to[:, pl.ds(part * depth, depth)] = a_ref[part, :, lanes]

    columns = o_ref.shape[2]
    for number in range(o_ref.shape[0]):
        at = pl.ds(number * columns, columns)
        total = sum(
            jnp.dot(
                a[...], w[:, :, at].reshape(parts * depth, columns), preferred_element_type=jnp.float32
            )
            for a, w in ((first, mine_ref), (second, other_ref))
        )
        o_ref[number] = total.astype(jnp.bfloat16)


def project(attended, mine, other, core):
    parts, rows, features = attended.shape
    depth = mine.shape[1]
    columns = mine.shape[2] // parts
    together = 4
    return pl.pallas_call(
        functools.partial(project_kernel, depth),
        out_shape=jax.ShapeDtypeStruct((parts, rows, columns), jnp.bfloat16),
        grid_spec=pltpu.PrefetchScalarGridSpec(
            num_scalar_prefetch=1,
            grid=(parts // together,),
            in_specs=[
                pl.BlockSpec((parts, rows, features), lambda i, t: (0, 0, 0)),
                pl.BlockSpec((parts, depth, together * columns), lambda i, t: (0, 0, i)),
                pl.BlockSpec((parts, depth, together * columns), lambda i, t: (0, 0, i)),
            ],
            out_specs=pl.BlockSpec((together, rows, columns), lambda i, t: (i, 0, 0)),
            scratch_shapes=[pltpu.VMEM((rows, parts * depth), jnp.bfloat16)] * 2,
        ),
        compiler_params=pltpu.CompilerParams(
            dimension_semantics=("arbitrary",), vmem_limit_bytes=32 * 1024 * 1024
        ),
        cost_estimate=pl.CostEstimate(
            flops=2 * parts * parts * rows * features * columns,
            bytes_accessed=2 * parts * parts * features * columns + 4 * parts * rows * features,
            transcendentals=0,
        ),
    )(core, attended, in_hbm(mine), in_hbm(other))


def join_kernel(key_ref, value_ref, o_ref):
    o_ref[:, :HEAD_SIZE] = key_ref[...]
    o_ref[:, HEAD_SIZE:] = value_ref[...]


def join(keys, values):
    rows = keys.shape[0]
    part = pl.BlockSpec((BLOCK_TOKENS, HEAD_SIZE), lambda i: (i, 0))
    return pl.pallas_call(
        join_kernel,
        out_shape=jax.ShapeDtypeStruct((rows, 2 * HEAD_SIZE), keys.dtype),
        grid=(rows // BLOCK_TOKENS,),
        in_specs=[part, part],
        out_specs=pl.BlockSpec((BLOCK_TOKENS, 2 * HEAD_SIZE), lambda i: (i, 0)),
    )(keys, values)


def half_kernel(core, w_ref, o_ref):
    o_ref[...] = w_ref[...]


def half_of(weight, core):
    rows, columns = weight.shape
    return pl.pallas_call(
        half_kernel,
        out_shape=jax.ShapeDtypeStruct((rows // 2, columns), weight.dtype),
        grid_spec=pltpu.PrefetchScalarGridSpec(
            num_scalar_prefetch=1,
            grid=(1,),
            in_specs=[pl.BlockSpec((rows // 2, columns), lambda i, core: (core[0], 0))],
            out_specs=pl.BlockSpec((rows // 2, columns), lambda i, core: (0, 0)),
        ),
    )(core, in_hbm(weight))


def gather_weight(out_weight, core):
    mine = half_of(out_weight, core[None])
    groups = [
        [((side ^ x_hi) * (CORES // 2) + rest) * 8 + x_hi * 4 + y for x_hi in range(2) for y in range(4)]
        for side in range(2)
        for rest in range(CORES // 2)
    ]
    return lax.all_gather(mine, ("ctx", "head"), axis=0, axis_index_groups=groups)


def per_device(queries, key_state_matrix, value_state_matrix, selected, out_weight):
    head_count = lax.axis_size("head")
    index = lax.axis_index("ctx")
    core = index % 2
    rows, width = queries.shape
    kv = join(key_state_matrix, value_state_matrix)
    other_selected = lax.ppermute(selected, "ctx", SWAP)
    mine = gather_weight(out_weight, core)
    chosen, row, place = exchange(kv, selected, other_selected, index)
    mine, chosen[-1] = lax.optimization_barrier((mine, chosen[-1]))
    other = lax.ppermute(mine, "ctx", SWAP)
    attended = attention(queries, kv, chosen, selected.reshape(-1), row, place)
    tokens = lax.all_to_all(
        attended.reshape(head_count, rows // head_count, width), "head", 0, 0, tiled=True
    )
    mixed = project(tokens, mine, other, core[None])
    return lax.all_to_all(mixed, "head", 0, 0, tiled=True).reshape(rows, -1)


def solution(mesh):
    return jax.shard_map(
        per_device,
        mesh=mesh,
        in_specs=(
            P("ctx", "head"),
            P("ctx", "head"),
            P("ctx", "head"),
            P("ctx", None),
            P("head", None),
        ),
        out_specs=P("ctx", "head"),
        check_vma=False,
    )
```

```python
import functools

import jax
import jax.numpy as jnp
import numpy as np
from jax import lax
from jax.experimental import pallas as pl
from jax.experimental.pallas import tpu as pltpu
from jax.sharding import PartitionSpec as P

HEAD_SIZE = 128
BLOCK_TOKENS = 512
TILE = 256
SLOTS = 4
BLOCKS = 4
ROWS = BLOCKS * BLOCK_TOKENS
RING = 8
CORES = 4 * RING
EXP2_SCALE = HEAD_SIZE ** (-0.5) * 1.4426950408889634

SCHEDULE = (
    (
        (
            0, 1, 2, 3, 4, 5, 6, -1, 8, -1, 10, -1, 12, -1, -1, 15,
            16, 17, 18, 19, 20, 21, 22, -1, 24, -1, 26, -1, 28, -1, -1, -1,
        ),
        (
            -1, 1, 2, -1, -1, 5, -1, 7, -1, 9, -1, 11, -1, 13, 14, -1,
            -1, -1, -1, -1, -1, -1, -1, -1, -1, -1, -1, -1, -1, -1, -1, -1,
        ),
    ),
    (
        (
            1, 0, 3, 2, 5, -1, 7, -1, 9, -1, 11, -1, 13, -1, -1, 14,
            17, 16, 19, 18, 21, -1, 23, -1, 25, -1, 27, -1, 29, -1, -1, -1,
        ),
        (
            -1, 0, 3, -1, -1, 4, -1, 6, -1, 8, -1, 10, -1, 12, 15, -1,
            -1, -1, -1, -1, -1, -1, -1, -1, -1, -1, -1, -1, -1, -1, -1, -1,
        ),
    ),
    (
        (
            -1, 3, 0, 5, 2, -1, 4, -1, 6, -1, 8, -1, 10, -1, -1, 1,
            -1, 19, 16, 21, 18, 5, 20, 7, 22, 9, 24, 11, 26, 13, 14, 17,
        ),
        (
            -1, 3, -1, -1, -1, -1, 4, -1, 6, -1, 8, -1, -1, 15, 12, -1,
            -1, -1, -1, -1, -1, -1, -1, -1, -1, -1, -1, -1, -1, -1, -1, -1,
        ),
    ),
    (
        (
            -1, 2, 1, -1, 3, -1, 5, -1, 7, -1, 9, -1, 11, -1, -1, 0,
            -1, 18, 17, -1, 19, 4, 21, 6, 23, 8, 25, 10, -1, 12, 15, 16,
        ),
        (
            -1, 2, -1, -1, -1, -1, -1, -1, -1, -1, 9, -1, -1, 14, 13, -1,
            -1, -1, -1, -1, -1, -1, -1, -1, -1, -1, -1, -1, -1, -1, -1, -1,
        ),
    ),
    (
        (
            -1, 5, -1, -1, 0, -1, 2, -1, 4, -1, 6, -1, 8, 1, -1, 3,
            14, 160, 35, 5, 16, 7, 18, 9, 20, 11, 22, 13, 952, 15, 12, 19,
        ),
        (
            -1, -1, 96, -1, 128, -1, 226, -1, 292, -1, 6, -1, 426, -1, 10, -1,
            -1, -1, -1, -1, -1, -1, -1, -1, -1, -1, -1, -1, -1, -1, -1, -1,
        ),
    ),
    (
        (
            -1, -1, -1, -1, 33, -1, 35, -1, 37, -1, 7, -1, 9, 0, -1, 2,
            15, 129, -1, 4, 17, 6, 51, 8, 21, 10, 23, 12, 57, 14, 13, 50,
        ),
        (
            -1, -1, -1, -1, 1, -1, 3, -1, 5, -1, 39, -1, -1, 96, 11, -1,
            -1, -1, -1, -1, -1, -1, -1, -1, -1, -1, -1, -1, -1, -1, -1, -1,
        ),
    ),
    (
        (
            -1, -1, -1, -1, -1, -1, 32, -1, 34, -1, 4, 1, 6, 3, -1, 37,
            12, 5, 14, 7, -1, 9, 48, 11, 50, 13, 20, 15, 54, 624, 10, -1,
        ),
        (
            -1, -1, -1, -1, -1, -1, 0, -1, 2, -1, 36, -1, 360, -1, 8, -1,
            -1, -1, -1, -1, -1, -1, -1, -1, -1, -1, -1, -1, -1, -1, -1, -1,
        ),
    ),
    (
        (
            -1, -1, -1, -1, -1, -1, -1, -1, -1, -1, -1, -1, 39, -1, -1, -1,
            45, 740, 47, 38, 33, 40, 611, 42, 37, 44, 742, 46, 55, 51, 43, -1,
        ),
        (
            -1, -1, -1, -1, -1, -1, -1, -1, -1, -1, -1, 96, -1, 162, 41, -1,
            -1, -1, -1, -1, -1, -1, -1, -1, -1, -1, -1, -1, -1, -1, -1, -1,
        ),
    ),
    (
        (
            -1, -1, -1, -1, -1, -1, -1, -1, -1, -1, -1, -1, 36, -1, -1, -1,
            42, 39, 44, 41, 46, 43, 32, 45, 34, 47, -1, -1, 52, -1, 40, 37,
        ),
        (
            -1, -1, -1, -1, -1, -1, -1, -1, -1, 33, -1, 35, 292, -1, 38, -1,
            -1, -1, -1, -1, -1, -1, -1, -1, -1, -1, -1, -1, -1, -1, -1, -1,
        ),
    ),
)
CHECKPOINTS = (4, 6, 7, 8)
COST = 12


def target(way, core):
    if way == 1:
        return core + CORES // 2
    side, place = divmod(core, CORES // 2)
    return side * (CORES // 2) + (place + (2 if core % 2 == 0 else -2)) % (CORES // 2)


def owners_of(item):
    if item < CORES:
        return [item] if item >= 0 else [], []
    second, first = divmod(item - CORES, CORES)
    return [], [first] + ([second - 1] if second else [])


def plan():
    found = [{core: "own", core ^ 1: "other"} for core in range(CORES)]
    parts = [{} for _ in range(CORES)]
    for step, sends in enumerate(SCHEDULE):
        for way, row in enumerate(sends):
            for core, item in enumerate(row):
                whole, wanted = owners_of(item)
                for owner in whole:
                    found[target(way, core)].setdefault(owner, (step, way))
                for position, owner in enumerate(wanted):
                    parts[target(way, core)].setdefault(owner, (step, way, position))
    return found, parts


def batches(found, parts):
    out = []
    for number, last in enumerate(CHECKPOINTS):
        first = -2 if number == 0 else CHECKPOINTS[number - 1]
        out.append(
            [
                [
                    owner
                    for owner, place in sorted((parts[core] | found[core]).items())
                    if (owner // 2 < core // 2 or owner == core ^ 1)
                    and first < (-1 if isinstance(place, str) else place[0]) <= last
                ]
                for core in range(CORES)
            ]
        )
    return out


def in_hbm(array):
    return pltpu.with_memory_space_constraint(array, pltpu.HBM)


def start_from(refs, numbers, source, first, rows, to, sem):
    for number in numbers:

        @pl.when(source == number)
        def _():
            at = pl.ds(pl.multiple_of(first, BLOCK_TOKENS), rows)
            pltpu.make_async_copy(refs[number].at[at], to, sem).start()


def wait_for(refs, source, rows, to, sem):
    @pl.when(source >= 0)
    def _():
        pltpu.make_async_copy(refs[0].at[pl.ds(0, rows)], to, sem).wait()


def move_kernel(ways, way_base, slots, slot_base, row, want, *refs):
    outs = len(ways) + (2 if slots else 0)
    ins, outs, sems = refs[: -outs - 1], refs[-outs - 1 : -1], refs[-1]

    def wanted(who, owner):
        return jnp.where(owner >= 0, want[who * CORES + jnp.maximum(owner, 0)], -1)

    jobs = []
    for way, (whole, *parts) in enumerate(ways):
        base = way_base + 5 * way
        if whole:
            jobs.append((whole, row[base], 0, ROWS, outs[way]))
        for position, numbers in enumerate(parts):
            for core in range(2 if numbers else 0):
                block = wanted(2 + 2 * way + core, row[base + 1 + 2 * position])
                to = outs[way].at[pl.ds((2 * position + core) * BLOCK_TOKENS, BLOCK_TOKENS)]
                source = jnp.where(block >= 0, row[base + 2 + 2 * position], -1)
                jobs.append((numbers, source, jnp.maximum(block, 0) * BLOCK_TOKENS, BLOCK_TOKENS, to))
    for slot, numbers in enumerate(slots):
        base = slot_base + 4 * slot
        for which in range(2):
            block = wanted(which, row[base])
            at = row[base + 2 + which]
            first = jnp.where(at >= 0, at, jnp.maximum(block, 0) * BLOCK_TOKENS)
            source = jnp.where(block >= 0, row[base + 1], -1)
            jobs.append((numbers, source, first, BLOCK_TOKENS, outs[len(ways) + which].at[slot]))
    for i, (numbers, source, first, rows, to) in enumerate(jobs):
        start_from(ins, numbers, source, first, rows, to, sems.at[i])
    for i, (numbers, source, first, rows, to) in enumerate(jobs):
        wait_for(ins, source, rows, to, sems.at[i])


def move(ways, slots, scalars, arrays, width, after=()):
    out_shapes = [(ROWS, width)] * len(ways[0]) + [(len(slots[0]), BLOCK_TOKENS, width)] * (2 if slots[0] else 0)

    def whole(shape):
        return pl.BlockSpec(shape, lambda *_: (0,) * len(shape))

    return pl.pallas_call(
        functools.partial(move_kernel, *ways, *slots),
        out_shape=[
            pltpu.HBM(s, arrays[0].dtype) if len(s) == 3 else jax.ShapeDtypeStruct(s, arrays[0].dtype)
            for s in out_shapes
        ],
        grid_spec=pltpu.PrefetchScalarGridSpec(
            num_scalar_prefetch=len(scalars),
            grid=(1,),
            in_specs=[pl.BlockSpec(memory_space=pltpu.HBM)] * (len(arrays) + len(after)),
            out_specs=[whole(s) for s in out_shapes],
            scratch_shapes=[pltpu.SemaphoreType.DMA((5 * len(ways[0]) + 2 * len(slots[0]),))],
        ),
        compiler_params=pltpu.CompilerParams(vmem_limit_bytes=24 * 1024 * 1024),
        cost_estimate=pl.CostEstimate(
            flops=0,
            bytes_accessed=4 * COST * sum(int(np.prod(s)) for s in out_shapes),
            transcendentals=0,
        ),
    )(*scalars, *arrays, *after)


class Plan:
    def __init__(self):
        found, parts = plan()
        groups = batches(found, parts)
        columns = []
        self.ways, self.slots, self.sources = {}, {}, {}

        def number_of(place, sources):
            if place not in sources:
                sources.append(place)
            return sources.index(place)

        def add(table):
            base = sum(c.shape[1] for c in columns)
            columns.append(table.reshape(CORES, -1))
            return base

        for step in range(1, len(SCHEDULE)):
            sources, numbers = self.sources.setdefault(step, []), []
            table = np.full((CORES, 2, 5), -1, np.int32)
            for way in range(2):
                used = [set(), set(), set()]
                for core, item in enumerate(SCHEDULE[step][way]):
                    whole, wanted = owners_of(item)
                    for owner in whole:
                        table[core, way, 0] = number_of(found[core][owner], sources)
                        used[0].add(int(table[core, way, 0]))
                    for i, owner in enumerate(wanted):
                        number = number_of(found[core][owner], sources)
                        table[core, way, 1 + 2 * i : 3 + 2 * i] = owner, number
                        used[1 + i].add(number)
                numbers.append(tuple(tuple(sorted(n)) for n in used))
            self.ways[step] = (tuple(numbers), add(table))

        held = np.full((CORES, CORES, 2), -1, np.int32)
        for batch, group in enumerate(groups):
            depth = max(len(owners) for owners in group)
            step = CHECKPOINTS[batch] + 2
            sources, numbers = self.sources.setdefault(step, []), [set() for _ in range(depth)]
            table = np.full((CORES, depth, 4), -1, np.int32)
            for core, owners in enumerate(group):
                for slot, owner in enumerate(owners):
                    held[core, owner] = (batch, slot)
                    if owner in found[core]:
                        number = number_of(found[core][owner], sources)
                        table[core, slot, :2] = owner, number
                    else:
                        *place, position = parts[core][owner]
                        number = number_of(tuple(place), sources)
                        rows = [(2 * position + c) * BLOCK_TOKENS for c in (core % 2, 1 - core % 2)]
                        table[core, slot] = owner, number, *rows
                    numbers[slot].add(number)
            self.slots[step] = (tuple(tuple(sorted(n)) for n in numbers), add(table))
        place = held.copy()
        for core in range(CORES):
            for owner in range(CORES):
                if held[core, owner, 0] < 0 <= held[core ^ 1, owner, 0]:
                    place[core, owner] = held[core ^ 1, owner]
                    place[core, owner, 0] += len(CHECKPOINTS)
        self.place = add(place)
        self.table = np.concatenate(columns, axis=1)


SWAP = [(i, i ^ 1) for i in range(CORES)]


def exchange(kv, selected, other_selected, index):
    tables = Plan()
    row = jnp.asarray(tables.table)[index]
    arrived = {"own": kv, "other": lax.ppermute(kv, "ctx", SWAP)}

    def pairs(step, way):
        return [(a, target(way, a)) for a, owner in enumerate(SCHEDULE[step][way]) if owner >= 0]

    mine, other = selected.reshape(1, -1), other_selected.reshape(1, -1)
    chip = jnp.where(index % 2 == 0, jnp.concatenate([mine, other]), jnp.concatenate([other, mine]))
    along, across = (
        lax.ppermute(chip, "ctx", [(target(way, i), i) for i in range(CORES >> way)]) for way in range(2)
    )
    choices = jnp.concatenate([mine, other, along, across])[:, None, :]
    owner = jnp.arange(CORES, dtype=jnp.int32)[None, :, None]
    named = (choices >= 0) & (choices // BLOCKS == owner)
    want = jnp.max(jnp.where(named, choices % BLOCKS, -1), axis=2).reshape(-1)

    kept, passed = [], []
    for step in range(CHECKPOINTS[-1] + 3):
        none = ((), 0)
        ways, slots = tables.ways.get(step, none), tables.slots.get(step, none)
        if step == 0:
            buffers = [kv, kv]
        elif ways[0] or slots[0]:
            buffers = move(
                ways,
                slots,
                [row, want if slots[0] or any(any(parts) for _, *parts in ways[0]) else row],
                [arrived[key] for key in tables.sources[step]],
                kv.shape[1],
                after=buffers[:1] if step <= len(SCHEDULE) else passed,
            )
        else:
            continue
        if step < len(SCHEDULE):
            for way in range(2):
                arrived[step, way] = lax.ppermute(buffers[way], "ctx", pairs(step, way))
        if slots[0]:
            keep, give = buffers[-2:]
            kept.append(keep)
            passed.append(lax.ppermute(give, "ctx", SWAP))
    return kept + passed, row, tables.place


def attention_kernel(q_heads, sources, place, info, row_ref, q_ref, kv_ref, *refs):
    chosen, (o_ref, keys, values, sems) = refs[:sources], refs[sources:]
    step = pl.program_id(0)
    steps = pl.num_programs(0)
    here = lax.rem(step, 2)
    own_to = pl.ds((SLOTS - 1) * BLOCK_TOKENS, BLOCK_TOKENS)

    def pair(block_ref, to, buf, slot):
        return (
            pltpu.make_async_copy(
                block_ref.at[:, pl.ds(0, HEAD_SIZE)], keys.at[buf, to], sems.at[buf, slot, 0]
            ),
            pltpu.make_async_copy(
                block_ref.at[:, pl.ds(HEAD_SIZE, HEAD_SIZE)],
                values.at[buf, to, pl.ds(0, HEAD_SIZE)],
                sems.at[buf, slot, 1],
            ),
        )

    def own_rows(at):
        return kv_ref.at[pl.ds(pl.multiple_of(at * BLOCK_TOKENS, BLOCK_TOKENS), BLOCK_TOKENS)]

    def choice(at, slot):
        block = info[at * (SLOTS - 1) + slot]
        owner = jnp.maximum(block, 0) // BLOCKS
        return jnp.where(block < 0, -1, row_ref[place + 2 * owner]), row_ref[place + 2 * owner + 1]

    def start(at, buf):
        for copy in pair(own_rows(at), own_to, buf, SLOTS - 1):
            copy.start()
        for slot in range(SLOTS - 1):
            to = pl.ds(slot * BLOCK_TOKENS, BLOCK_TOKENS)
            array, block = choice(at, slot)
            for number in range(sources):

                @pl.when(array == number)
                def _():
                    for copy in pair(chosen[number].at[block], to, buf, slot):
                        copy.start()

    @pl.when(step == 0)
    def _():
        start(step, here)

    @pl.when(step + 1 < steps)
    def _():
        start(step + 1, 1 - here)

    values[here, :, pl.ds(HEAD_SIZE, HEAD_SIZE)] = jnp.ones(
        (SLOTS * BLOCK_TOKENS, HEAD_SIZE), jnp.bfloat16
    )
    for copy in pair(own_rows(step), own_to, here, SLOTS - 1):
        copy.wait()
    for slot in range(SLOTS - 1):
        to = pl.ds(slot * BLOCK_TOKENS, BLOCK_TOKENS)
        array, _ = choice(step, slot)

        @pl.when(array >= 0)
        def _():
            for copy in pair(own_rows(step), to, here, slot):
                copy.wait()

        @pl.when(array < 0)
        def _():
            first = keys[here, pl.ds((SLOTS - 1) * BLOCK_TOKENS, 16), :][0:1, :]
            keys[here, to, :] = jnp.broadcast_to(first, (BLOCK_TOKENS, HEAD_SIZE))
            values[here, to, :] = jnp.zeros((BLOCK_TOKENS, 2 * HEAD_SIZE), jnp.bfloat16)

    row = lax.broadcasted_iota(jnp.int32, (TILE, TILE), 0)
    col = lax.broadcasted_iota(jnp.int32, (TILE, TILE), 1)
    causal = row >= col
    dims = (((1,), (1,)), ((), ()))

    units = [(head, tile) for head in range(q_heads) for tile in range(BLOCK_TOKENS // TILE)]

    def places(unit):
        head, tile = unit
        far = (SLOTS - 1) * BLOCK_TOKENS + tile * TILE
        return pl.ds(tile * TILE, TILE), pl.ds(head * HEAD_SIZE, HEAD_SIZE), pl.ds(0, far), pl.ds(far, TILE)

    def scores(unit):
        rows, lanes, *parts = places(unit)
        query = q_ref[rows, lanes]
        far, near = (
            lax.dot_general(query, keys[here, at, :], dims, preferred_element_type=jnp.float32)
            for at in parts
        )
        return far, jnp.where(causal, near, -1e30)

    following = scores(units[0])
    for number, unit in enumerate(units):
        now = following
        if number + 1 < len(units):
            following = scores(units[number + 1])
        rows, lanes, *parts = places(unit)
        highest = functools.reduce(jnp.maximum, [jnp.max(s, axis=1, keepdims=True) for s in now])
        total = sum(
            jnp.dot(
                jnp.exp2((s - highest) * EXP2_SCALE).astype(jnp.bfloat16),
                values[here, at, :],
                preferred_element_type=jnp.float32,
            )
            for s, at in zip(now, parts)
        )
        o_ref[rows, lanes] = (total[:, :HEAD_SIZE] / total[:, HEAD_SIZE:]).astype(jnp.bfloat16)


def attention(queries, kv, chosen, info, row, place):
    rows, width = queries.shape
    blocks = rows // BLOCK_TOKENS
    keys = SLOTS * BLOCK_TOKENS
    return pl.pallas_call(
        functools.partial(attention_kernel, width // HEAD_SIZE, len(chosen), place),
        out_shape=jax.ShapeDtypeStruct((rows, width), jnp.bfloat16),
        grid_spec=pltpu.PrefetchScalarGridSpec(
            num_scalar_prefetch=2,
            grid=(blocks,),
            in_specs=[pl.BlockSpec((BLOCK_TOKENS, width), lambda i, *_: (i, 0))]
            + [pl.BlockSpec(memory_space=pltpu.HBM)] * (1 + len(chosen)),
            out_specs=pl.BlockSpec((BLOCK_TOKENS, width), lambda i, *_: (i, 0)),
            scratch_shapes=[
                pltpu.VMEM((2, keys, HEAD_SIZE), jnp.bfloat16),
                pltpu.VMEM((2, keys, 2 * HEAD_SIZE), jnp.bfloat16),
                pltpu.SemaphoreType.DMA((2, SLOTS, 2)),
            ],
        ),
        compiler_params=pltpu.CompilerParams(
            dimension_semantics=("arbitrary",), vmem_limit_bytes=48 * 1024 * 1024
        ),
        cost_estimate=pl.CostEstimate(
            flops=4 * rows * (width // HEAD_SIZE) * keys * HEAD_SIZE,
            bytes_accessed=4 * rows * width + 4 * blocks * keys * HEAD_SIZE,
            transcendentals=rows * (width // HEAD_SIZE) * keys,
        ),
    )(info, row, *map(in_hbm, (queries, kv, *chosen)))


def project_kernel(depth, core, a_ref, mine_ref, other_ref, o_ref, first, second):
    parts, rows, _ = a_ref.shape

    @pl.when(pl.program_id(0) == 0)
    def _():
        for to, half in ((first, core[0]), (second, 1 - core[0])):
            lanes = pl.ds(pl.multiple_of(half * depth, depth), depth)
            for part in range(parts):
                to[:, pl.ds(part * depth, depth)] = a_ref[part, :, lanes]

    columns = o_ref.shape[2]
    for number in range(o_ref.shape[0]):
        at = pl.ds(number * columns, columns)
        total = sum(
            jnp.dot(
                a[...], w[:, :, at].reshape(parts * depth, columns), preferred_element_type=jnp.float32
            )
            for a, w in ((first, mine_ref), (second, other_ref))
        )
        o_ref[number] = total.astype(jnp.bfloat16)


def project(attended, mine, other, core):
    parts, rows, features = attended.shape
    depth = mine.shape[1]
    columns = mine.shape[2] // parts
    together = 4
    return pl.pallas_call(
        functools.partial(project_kernel, depth),
        out_shape=jax.ShapeDtypeStruct((parts, rows, columns), jnp.bfloat16),
        grid_spec=pltpu.PrefetchScalarGridSpec(
            num_scalar_prefetch=1,
            grid=(parts // together,),
            in_specs=[
                pl.BlockSpec((parts, rows, features), lambda i, t: (0, 0, 0)),
                pl.BlockSpec((parts, depth, together * columns), lambda i, t: (0, 0, i)),
                pl.BlockSpec((parts, depth, together * columns), lambda i, t: (0, 0, i)),
            ],
            out_specs=pl.BlockSpec((together, rows, columns), lambda i, t: (i, 0, 0)),
            scratch_shapes=[pltpu.VMEM((rows, parts * depth), jnp.bfloat16)] * 2,
        ),
        compiler_params=pltpu.CompilerParams(
            dimension_semantics=("arbitrary",), vmem_limit_bytes=32 * 1024 * 1024
        ),
        cost_estimate=pl.CostEstimate(
            flops=2 * parts * parts * rows * features * columns,
            bytes_accessed=2 * parts * parts * features * columns + 4 * parts * rows * features,
            transcendentals=0,
        ),
    )(core, attended, in_hbm(mine), in_hbm(other))


def gather_weight(out_weight, core):
    half = out_weight.shape[0] // 2
    mine = lax.dynamic_slice_in_dim(out_weight, core * half, half, 0)
    groups = [
        [((side ^ x_hi) * (CORES // 2) + rest) * 8 + x_hi * 4 + y for x_hi in range(2) for y in range(4)]
        for side in range(2)
        for rest in range(CORES // 2)
    ]
    return lax.all_gather(mine, ("ctx", "head"), axis=0, axis_index_groups=groups)


def per_device(queries, key_state_matrix, value_state_matrix, selected, out_weight):
    head_count = lax.axis_size("head")
    index = lax.axis_index("ctx")
    core = index % 2
    rows, width = queries.shape
    kv = jnp.concatenate([key_state_matrix, value_state_matrix], axis=1)
    other_selected = lax.ppermute(selected, "ctx", SWAP)
    mine = gather_weight(out_weight, core)
    chosen, row, place = exchange(kv, selected, other_selected, index)
    mine, chosen[-1] = lax.optimization_barrier((mine, chosen[-1]))
    other = lax.ppermute(mine, "ctx", SWAP)
    attended = attention(queries, kv, chosen, selected.reshape(-1), row, place)
    tokens = lax.all_to_all(
        attended.reshape(head_count, rows // head_count, width), "head", 0, 0, tiled=True
    )
    mixed = project(tokens, mine, other, core[None])
    return lax.all_to_all(mixed, "head", 0, 0, tiled=True).reshape(rows, -1)


def solution(mesh):
    return jax.shard_map(
        per_device,
        mesh=mesh,
        in_specs=(
            P("ctx", "head"),
            P("ctx", "head"),
            P("ctx", "head"),
            P("ctx", None),
            P("head", None),
        ),
        out_specs=P("ctx", "head"),
        check_vma=False,
    )
```
